512 devices in a mesh: rep: 4 (over x), shard: 128 (over y, z, core).
Axes of the slice: x: 4, y: 8, z: 8, core: 2. Of those that a mesh axis runs over, the one named last changes fastest.
Arguments:
- partials: bfloat16 [4, 224, 512, 512], P('rep', None, 'shard'), may hold values from -0.41992188 to 0.41992188
- owners: int32 [224], replicated, may hold values from 0 to 127, as said below
- left_stat: bfloat16 [128, 4, 512, 512], P('shard', None, 'rep'), may hold values from -6 to 6
- right_stat: bfloat16 [128, 4, 512, 512], P('shard', None, 'rep'), may hold values from -6 to 6
- left_factor: bfloat16 [128, 4, 512, 512], P('shard', None, 'rep'), may hold values from -0.2 to 3.2
- right_factor: bfloat16 [128, 4, 512, 512], P('shard', None, None, 'rep'), may hold values from -0.2 to 3.2
Outputs:
- left_stat_new: bfloat16 [128, 4, 512, 512], P('shard', None, 'rep')
- right_stat_new: bfloat16 [128, 4, 512, 512], P('shard', None, 'rep')
- update: bfloat16 [224, 512, 512], P(None, 'shard', 'rep')
The draws below stay inside these ranges and needn't reach their ends.
Inputs may be any that keep to these rules, and one draw needn't show every extreme that they name: `owners`: each owner holds at most 4 blocks, and some owner holds exactly 4.
All inputs are finite; a program needn't handle non-finite values.
Results may differ from the reference program's by a relative error of at most 0.017.
Values may be sent and summed in bfloat16 or wider, within the bound.
No kernel may reach another device: no remote copies, remote signals or barrier semaphores. Data moves between devices by JAX's collectives and lax.ppermute only.
A program may use at most 64 MiB of HBM per device.

```python
import jax
import jax.numpy as jnp
from jax import lax

B = 512
CAP = 4
NBLK = 224
N_REP = 4
N_SHARD = 128


def factor_matrix(off_part, diag_part):
    rows = lax.broadcasted_iota(jnp.int32, off_part.shape, off_part.ndim - 2)
    cols = lax.broadcasted_iota(jnp.int32, off_part.shape, off_part.ndim - 1)
    return jnp.where(rows == cols, diag_part, off_part)


def draw_owners(key, part):
    key = jax.random.fold_in(key, 11)
    busy_key = jax.random.fold_in(key, 1)
    popular_key = jax.random.fold_in(key, 2)
    noise_key = jax.random.fold_in(key, 3)
    shuffle_key = jax.random.fold_in(key, 4)
    busy = jax.random.randint(busy_key, (), 0, N_SHARD)
    others = (busy + 1 + jnp.arange(N_SHARD - 1)) % N_SHARD
    popular = jax.random.randint(popular_key, (N_SHARD - 1,), 0, 4)
    copies = CAP - 1
    owner_of = jnp.repeat(others, copies)
    copy_index = jnp.tile(jnp.arange(copies), N_SHARD - 1)
    noise = jax.random.randint(noise_key, owner_of.shape, 0, 1000)
    score = (noise + 700 * jnp.repeat(popular, copies) - 400 * copy_index) * 65536 + jnp.arange(owner_of.shape[0])
    _, picked = lax.top_k(score, NBLK - CAP)
    chosen = owner_of[picked]
    whole = jnp.concatenate([jnp.full((CAP,), busy, jnp.int32), chosen.astype(jnp.int32)])
    shuffle = jax.random.permutation(shuffle_key, NBLK)
    return whole[shuffle].astype(jnp.int32)


def draw_left_factor(key, part):
    key = jax.random.fold_in(key, 21)
    off_key = jax.random.fold_in(key, 1)
    diag_key = jax.random.fold_in(key, 2)
    shape = (N_SHARD, CAP, B, B)
    off_part = jnp.clip(jax.random.normal(off_key, shape, jnp.float32), -4.0, 4.0) * 0.044
    diag_part = jnp.exp(jax.random.uniform(diag_key, shape, jnp.float32, 0.405, 1.098))
    return factor_matrix(off_part, diag_part).astype(jnp.bfloat16)


def draw_right_factor(key, part):
    key = jax.random.fold_in(key, 31)
    off_key = jax.random.fold_in(key, 1)
    diag_key = jax.random.fold_in(key, 2)
    shape = (N_SHARD, CAP, B, B)
    off_part = jnp.clip(jax.random.normal(off_key, shape, jnp.float32), -4.0, 4.0) * 0.044
    diag_part = jnp.exp(jax.random.uniform(diag_key, shape, jnp.float32, 0.405, 1.098))
    return factor_matrix(off_part, diag_part).astype(jnp.bfloat16)


def block_levels(key, dims, pieces, low, largest):
    gain = 1.0
    for axis_at, blocks in pieces:
        steps = jax.random.uniform(jax.random.fold_in(jax.random.fold_in(key, 6), axis_at), (blocks,), jnp.float32, low / len(pieces), largest / len(pieces))
        gain = gain * jnp.repeat(jnp.exp(steps), dims[axis_at] // blocks).reshape((-1,) + (1,) * (len(dims) - 1 - axis_at))
    return gain


def gaussian(rng, dims, deviation, reach, pieces=(), held_as=jnp.bfloat16):
    values = jax.random.normal(rng, dims, jnp.float32) * deviation
    if len(pieces) > 0:
        values = block_levels(rng, dims, pieces, -0.22, 0.18) * values
    return jnp.clip(values, min=-reach, max=reach).astype(held_as)


def setup_inputs(seed: int = 0) -> dict:
    splits = jax.random.split(jax.random.key(seed), 7)
    return {
        "partials": gaussian(splits[0], (N_REP, NBLK, B, B), 0.07, 0.41992188, ((0, 4), (2, 128))),
        "owners": draw_owners(jax.random.fold_in(splits[6], 71), 0),
        "left_stat": gaussian(splits[2], (N_SHARD, CAP, B, B), 1.0, 6.0, ((0, 128), (2, 4))),
        "right_stat": gaussian(splits[3], (N_SHARD, CAP, B, B), 1.0, 6.0, ((0, 128), (2, 4))),
        "left_factor": draw_left_factor(jax.random.fold_in(splits[6], 71), 0),
        "right_factor": draw_right_factor(jax.random.fold_in(splits[6], 71), 0),
    }


def slots_of(owners):
    count = owners.shape[0]
    same_owner = owners[:, None] == owners[None, :]
    before = jnp.arange(count)[None, :] < jnp.arange(count)[:, None]
    return jnp.sum(jnp.where(same_owner & before, 1, 0), axis=1).astype(jnp.int32)


def per_block(inputs):
    grad_block, left_block, right_block = inputs
    left_upd = jnp.dot(grad_block, grad_block.T, preferred_element_type=jnp.float32)
    right_upd = jnp.dot(grad_block.T, grad_block, preferred_element_type=jnp.float32)
    left_product = jnp.dot(left_block, grad_block, preferred_element_type=jnp.float32).astype(jnp.bfloat16)
    result = jnp.dot(left_product, right_block, preferred_element_type=jnp.float32).astype(jnp.bfloat16)
    return left_upd, right_upd, result


def reference(partials, owners, left_stat, right_stat, left_factor, right_factor):
    total = partials[0].astype(jnp.float32)
    for replica in range(1, N_REP):
        total = total + partials[replica].astype(jnp.float32)
    grad = total.astype(jnp.bfloat16)
    slot = slots_of(owners)
    left_blocks = left_factor[owners, slot]
    right_blocks = right_factor[owners, slot]
    left_upds, right_upds, update = lax.map(per_block, (grad, left_blocks, right_blocks))
    left_new = (0.9 * left_stat.astype(jnp.float32)).at[owners, slot].add(0.1 * left_upds)
    right_new = (0.9 * right_stat.astype(jnp.float32)).at[owners, slot].add(0.1 * right_upds)
    return left_new.astype(jnp.bfloat16), right_new.astype(jnp.bfloat16), update
```

```python
import functools

import jax
import jax.numpy as jnp
from jax import lax
from jax.experimental import pallas as pl
from jax.experimental.pallas import tpu as pltpu
from jax.sharding import PartitionSpec as P

VMEM = pltpu.VMEM
LIMIT = 48 * 1024 * 1024
F32 = jnp.float32
BF16 = jnp.bfloat16


def params(**kw):
    return pltpu.CompilerParams(vmem_limit_bytes=LIMIT, **kw)


def whole():
    return pl.BlockSpec(memory_space=VMEM)


def smem():
    return pl.BlockSpec(memory_space=pltpu.SMEM)


def pack_kernel(order_ref, slot_ref, part_ref, factor_ref, out_ref):
    classes, size = out_ref.shape[0], out_ref.shape[1]
    panel = factor_ref.shape[1]
    count = size - panel
    for c in range(classes):

        def move(j, _):
            out_ref[c, j] = part_ref[order_ref[c * count + j]]
            return 0

        lax.fori_loop(0, count, move, 0, unroll=8)
        out_ref[c, pl.ds(count, panel)] = factor_ref[slot_ref[c]]


def spread_kernel(owner_ref, in_ref, out_ref):
    out_ref[...] = jnp.zeros_like(out_ref)
    count = owner_ref.shape[0]

    def add(j, _):
        total = in_ref[0, j].astype(F32)
        for r in range(1, in_ref.shape[0]):
            total = total + in_ref[r, j].astype(F32)
        out_ref[owner_ref[j]] = total.astype(out_ref.dtype)
        return 0

    lax.fori_loop(0, count, add, 0, unroll=4)


def update_kernel(slot_ref, left_ref, grad_ref, right_ref, out_ref):
    del slot_ref
    panels = grad_ref.shape[0]
    grad = jnp.concatenate([grad_ref[c] for c in range(panels)], axis=1)
    right = jnp.concatenate([right_ref[c] for c in range(panels)], axis=1)
    rows = left_ref.shape[2]
    for r in range(left_ref.shape[0]):
        product = jnp.dot(left_ref[r, 0], grad, preferred_element_type=F32).astype(BF16)
        result = jnp.dot(product, right, preferred_element_type=F32).astype(BF16)
        for c in range(panels):
            out_ref[c, pl.ds(r * rows, rows), :] = result[:, c * 128 : (c + 1) * 128]


def stats_kernel(meta_ref, grad_ref, left_ref, right_ref, left_out, right_out):
    replica = meta_ref[4]
    panels = grad_ref.shape[1]
    rows = left_ref.shape[2]
    start = pl.multiple_of(replica * rows, rows)
    grad = jnp.concatenate([grad_ref[0, c] for c in range(panels)], axis=1)
    own_rows = jnp.concatenate([grad_ref[0, c, pl.ds(start, rows), :] for c in range(panels)], axis=1)
    own_cols = grad_ref[0, replica]
    left = lax.dot_general(own_rows, grad, (((1,), (1,)), ((), ())), preferred_element_type=F32)
    right = lax.dot_general(own_cols, grad, (((0,), (0,)), ((), ())), preferred_element_type=F32)
    left_out[0, 0] = (0.9 * left_ref[0, 0].astype(F32) + 0.1 * left).astype(left_out.dtype)
    right_out[0, 0] = (0.9 * right_ref[0, 0].astype(F32) + 0.1 * right).astype(right_out.dtype)


def collect_kernel(source_ref, in_ref, out_ref):
    def move(b, _):
        out_ref[b] = in_ref[source_ref[b]]
        return 0

    lax.fori_loop(0, out_ref.shape[0], move, 0, unroll=8)


def per_device(partials, owners, left_stat, right_stat, left_factor, right_factor):
    shards = lax.axis_size("shard")
    classes = lax.axis_size("rep")
    replica = lax.axis_index("rep")
    me = lax.axis_index("shard")
    _, blocks, rows, width = partials.shape
    slots = left_stat.shape[1]
    quarter = width // classes
    lanes = quarter
    panels = width // lanes
    per_class = blocks // classes
    tile = rows * panels

    number = jnp.arange(blocks, dtype=jnp.int32)
    key = owners * blocks + number
    position = jnp.sum((key[None, :] < key[:, None]).astype(jnp.int32), axis=1)
    place = (position % classes) * per_class + position // classes
    order = jnp.sum(jnp.where(place[None, :] == number[:, None], number[None, :], 0), axis=1)
    class_owner = jnp.sum(
        jnp.where(
            position[None, :] == (number[:per_class] * classes + replica)[:, None], owners[None, :], 0
        ),
        axis=1,
    )
    source = (position % classes) * shards + owners
    base = jnp.sum((owners < me).astype(jnp.int32))
    each = jnp.arange(classes, dtype=jnp.int32)
    slot_of_class = (each + 4 * classes - base % classes) % classes
    class_of_slot = (each + base) % classes
    my_slot = (replica + classes - base % classes) % classes

    left_all = lax.all_gather(left_factor[0], "rep", axis=0, tiled=False)

    part_tiles = (
        partials[0].reshape(blocks, rows, panels, lanes).transpose(0, 2, 1, 3).reshape(blocks, tile, lanes)
    )
    factor_tiles = right_factor[0].reshape(slots, width // tile, tile, quarter)
    size = per_class + width // tile
    message = pl.pallas_call(
        pack_kernel,
        out_shape=jax.ShapeDtypeStruct((classes, size, tile, lanes), BF16),
        in_specs=[smem(), smem(), whole(), whole()],
        out_specs=whole(),
        compiler_params=params(),
        name="pack",
    )(order, slot_of_class, part_tiles, factor_tiles)
    received = lax.all_to_all(message, "rep", split_axis=0, concat_axis=0, tiled=True)
    right_panels = received[:, per_class:].reshape(classes, width, lanes)
    outgoing = pl.pallas_call(
        spread_kernel,
        out_shape=jax.ShapeDtypeStruct((shards, tile, lanes), BF16),
        in_specs=[smem(), whole()],
        out_specs=whole(),
        compiler_params=params(),
        name="spread",
    )(class_owner, received)
    incoming = lax.all_to_all(outgoing, "shard", split_axis=0, concat_axis=0, tiled=True)
    grad = (
        incoming.reshape(shards, panels, rows, lanes).transpose(1, 0, 2, 3).reshape(panels, width, lanes)
    )
    grads = lax.all_gather(grad, "rep", axis=0, tiled=False)

    update_panels = pl.pallas_call(
        update_kernel,
        out_shape=jax.ShapeDtypeStruct((panels, width, lanes), BF16),
        grid_spec=pltpu.PrefetchScalarGridSpec(
            num_scalar_prefetch=1,
            grid=(1,),
            in_specs=[
                pl.BlockSpec((classes, 1, quarter, width), lambda i, s: (0, s[0], 0, 0)),
                pl.BlockSpec((panels, width, lanes), lambda i, s: (0, 0, 0)),
                pl.BlockSpec((panels, width, lanes), lambda i, s: (0, 0, 0)),
            ],
            out_specs=pl.BlockSpec((panels, width, lanes), lambda i, s: (0, 0, 0)),
        ),
        compiler_params=params(),
        cost_estimate=pl.CostEstimate(flops=4 * width**3, bytes_accessed=8 * width**2, transcendentals=0),
        name="update",
    )(my_slot[None], left_all, grad, right_panels)
    returned = lax.all_to_all(
        update_panels.reshape(panels * shards, rows, lanes),
        ("rep", "shard"),
        split_axis=0,
        concat_axis=0,
        tiled=True,
    )
    update = pl.pallas_call(
        collect_kernel,
        out_shape=jax.ShapeDtypeStruct((blocks, rows, lanes), BF16),
        in_specs=[smem(), whole()],
        out_specs=whole(),
        compiler_params=params(),
        name="collect",
    )(source, returned)

    stat_spec = pl.BlockSpec((1, 1, quarter, width), lambda k, s: (0, k, 0, 0))
    left_new, right_new = pl.pallas_call(
        stats_kernel,
        out_shape=(
            jax.ShapeDtypeStruct(left_stat.shape, BF16),
            jax.ShapeDtypeStruct(right_stat.shape, BF16),
        ),
        grid_spec=pltpu.PrefetchScalarGridSpec(
            num_scalar_prefetch=1,
            grid=(slots,),
            in_specs=[
                pl.BlockSpec((1, panels, width, lanes), lambda k, s: (s[k], 0, 0, 0)),
                stat_spec,
                stat_spec,
            ],
            out_specs=[stat_spec, stat_spec],
        ),
        compiler_params=params(),
        cost_estimate=pl.CostEstimate(
            flops=4 * slots * quarter * width**2, bytes_accessed=16 * slots * quarter * width, transcendentals=0
        ),
        name="stats",
    )(jnp.concatenate([class_of_slot, replica[None]]), grads, left_stat, right_stat)
    return left_new, right_new, update


def solution(mesh):
    return jax.shard_map(
        per_device,
        mesh=mesh,
        in_specs=(
            P("rep", None, "shard", None),
            P(),
            P("shard", None, "rep", None),
            P("shard", None, "rep", None),
            P("shard", None, "rep", None),
            P("shard", None, None, "rep"),
        ),
        out_specs=(
            P("shard", None, "rep", None),
            P("shard", None, "rep", None),
            P(None, "shard", "rep"),
        ),
        check_vma=False,
    )
```

```python
import jax
import jax.numpy as jnp
from jax import lax
from jax.experimental import pallas as pl
from jax.experimental.pallas import tpu as pltpu
from jax.sharding import PartitionSpec as P

VMEM = pltpu.VMEM
SMEM = pltpu.SMEM
LIMIT = 40 * 1024 * 1024
WIDE = 58 * 1024 * 1024
F32 = jnp.float32
BF16 = jnp.bfloat16
LANES = 128
TILE = 16


def params(limit=LIMIT):
    return pltpu.CompilerParams(vmem_limit_bytes=limit)


def in_vmem():
    return pl.BlockSpec(memory_space=VMEM)


def in_smem():
    return pl.BlockSpec(memory_space=SMEM)


def anywhere():
    return pl.BlockSpec(memory_space=pl.ANY)


def pack_kernel(
    where_ref, owners_ref, lanes_ref, part_ref, left_ref, right_ref,
    out_ref, owner_at_ref, source_ref, base_ref,
    part, left, rank, rank_at, sems,
):
    classes = out_ref.shape[0]
    blocks = part_ref.shape[0]
    count = blocks // classes
    shards = where_ref[2]
    me = where_ref[0]
    panel = right_ref.shape[1]
    side = left_ref.shape[1]
    load_part = pltpu.make_async_copy(part_ref, part, sems.at[0])
    load_left = pltpu.make_async_copy(left_ref, left, sems.at[1])
    load_part.start()
    load_left.start()

    key = lanes_ref[...] * blocks + lax.broadcasted_iota(jnp.int32, lanes_ref.shape, 1)

    def compare(b, carry):
        before, base = carry
        owner = owners_ref[b]
        before = before + jnp.where(key > owner * blocks + b, 1, 0)
        return before, base + jnp.where(owner < me, 1, 0)

    before, base = lax.fori_loop(
        0, blocks, compare, (jnp.zeros_like(key), jnp.int32(0)), unroll=8
    )
    rank[...] = before
    base_ref[0] = base
    place = pltpu.make_async_copy(rank, rank_at, sems.at[2])
    place.start()
    loads = []
    slots = []
    for c in range(classes):
        slot = lax.rem(c + classes - lax.rem(base, classes), classes)
        load = pltpu.make_async_copy(right_ref.at[slot], out_ref.at[c, pl.ds(count, panel)], sems.at[3 + c])
        load.start()
        loads.append(load)
        slots.append(slot)
    load_left.wait()
    for c in range(classes):
        for h in range(left.shape[2] // LANES):
            rows = left[slots[c], :, h * LANES : (h + 1) * LANES]
            out_ref[c, pl.ds(count + panel + h * side // TILE, side // TILE)] = rows.reshape(
                side // TILE, TILE, LANES
            )
    place.wait()
    load_part.wait()

    def move(b, _):
        p = rank_at[0, b]
        c = lax.rem(p, classes)
        j = lax.div(p, classes)
        out_ref[c, j] = part[b]
        owner = owners_ref[b]
        owner_at_ref[c * count + j] = owner
        source_ref[b] = c * shards + owner
        return 0

    lax.fori_loop(0, blocks, move, 0, unroll=8)
    for load in loads:
        load.wait()


def spread_kernel(where_ref, owner_at_ref, in_ref, out_ref):
    out_ref[...] = jnp.zeros_like(out_ref)
    classes = in_ref.shape[0]
    count = owner_at_ref.shape[0] // classes
    first = where_ref[1] * count

    def add(j, _):
        total = in_ref[0, j].astype(F32)
        for r in range(1, classes):
            total = total + in_ref[r, j].astype(F32)
        out_ref[owner_at_ref[first + j]] = total.astype(out_ref.dtype)
        return 0

    lax.fori_loop(0, count, add, 0, unroll=8)


def update_kernel(count, grad_ref, in_ref, out_ref, copy_ref, sem):
    hand_on = pltpu.make_async_copy(grad_ref, copy_ref, sem)
    hand_on.start()
    panels, width, _ = grad_ref.shape
    rows = width // panels
    tall = width // TILE
    wide = rows // TILE
    grad = jnp.concatenate([grad_ref[c] for c in range(panels)], axis=1)
    right = jnp.concatenate(
        [in_ref[c, pl.ds(count, tall)].reshape(width, LANES) for c in range(panels)], axis=1
    )
    for r in range(panels):
        left = jnp.concatenate(
            [
                in_ref[r, pl.ds(count + tall + h * wide, wide)].reshape(rows, LANES)
                for h in range(width // LANES)
            ],
            axis=1,
        )
        product = jnp.dot(left, grad, preferred_element_type=F32).astype(BF16)
        result = jnp.dot(product, right, preferred_element_type=F32).astype(BF16)
        for c in range(panels):
            out_ref[c, pl.ds(r * rows, rows), :] = result[:, c * LANES : (c + 1) * LANES]
    hand_on.wait()


def finish_kernel(
    where_ref, source_ref, base_ref, in_ref, grads_ref, left_ref, right_ref,
    left_out, right_out, update_out,
    grads, lefts, rights, update, in_sems, out_sems,
):
    slots, rows, _ = left_ref.shape
    panels = grads_ref.shape[1]
    replica = where_ref[1]
    base = base_ref[0]
    loads = []
    for k in range(slots):
        c = lax.rem(base + k, slots)
        step = [
            pltpu.make_async_copy(grads_ref.at[c], grads.at[k], in_sems.at[k, 0]),
            pltpu.make_async_copy(left_ref.at[k], lefts.at[k], in_sems.at[k, 1]),
            pltpu.make_async_copy(right_ref.at[k], rights.at[k], in_sems.at[k, 2]),
        ]
        for load in step:
            load.start()
        loads.append(step)

    def move(b, _):
        update[b] = in_ref[source_ref[b]]
        return 0

    lax.fori_loop(0, update.shape[0], move, 0, unroll=8)
    stores = [pltpu.make_async_copy(update, update_out, out_sems.at[2 * slots])]
    stores[0].start()
    start = pl.multiple_of(replica * rows, rows)
    for k in range(slots):
        for load in loads[k]:
            load.wait()
        grad = jnp.concatenate([grads[k, c] for c in range(panels)], axis=1)
        own_rows = jnp.concatenate([grads[k, c, pl.ds(start, rows), :] for c in range(panels)], axis=1)
        own_cols = grads[k, replica]
        left = lax.dot_general(own_rows, grad, (((1,), (1,)), ((), ())), preferred_element_type=F32)
        right = lax.dot_general(own_cols, grad, (((0,), (0,)), ((), ())), preferred_element_type=F32)
        lefts[k] = (0.9 * lefts[k].astype(F32) + 0.1 * left).astype(lefts.dtype)
        rights[k] = (0.9 * rights[k].astype(F32) + 0.1 * right).astype(rights.dtype)
        for n, (new, out) in enumerate(((lefts, left_out), (rights, right_out))):
            store = pltpu.make_async_copy(new.at[k], out.at[k], out_sems.at[2 * k + n])
            store.start()
            stores.append(store)
    for store in stores:
        store.wait()


def per_device(partials, owners, left_stat, right_stat, left_factor, right_factor):
    shards = lax.axis_size("shard")
    classes = lax.axis_size("rep")
    where = jnp.stack([lax.axis_index("shard"), lax.axis_index("rep"), jnp.int32(shards)])
    _, blocks, rows, width = partials.shape
    slots = left_stat.shape[1]
    quarter = width // classes
    panels = width // LANES
    count = blocks // classes
    tall = width // TILE
    size = count + 2 * tall

    part_tiles = (
        partials[0].reshape(blocks, rows, panels, LANES).transpose(0, 2, 1, 3).reshape(blocks, TILE, LANES)
    )
    right_tiles = right_factor[0].reshape(slots, tall, TILE, LANES)
    message, owner_at, source, base = pl.pallas_call(
        pack_kernel,
        out_shape=(
            jax.ShapeDtypeStruct((classes, size, TILE, LANES), BF16),
            jax.ShapeDtypeStruct((blocks,), jnp.int32),
            jax.ShapeDtypeStruct((blocks,), jnp.int32),
            jax.ShapeDtypeStruct((1,), jnp.int32),
        ),
        in_specs=[in_smem(), in_smem(), in_vmem(), anywhere(), anywhere(), anywhere()],
        out_specs=(in_vmem(), in_smem(), in_smem(), in_smem()),
        scratch_shapes=[
            VMEM((blocks, TILE, LANES), BF16),
            VMEM((slots, quarter, width), BF16),
            VMEM((1, blocks), jnp.int32),
            SMEM((1, blocks), jnp.int32),
            pltpu.SemaphoreType.DMA((3 + classes,)),
        ],
        compiler_params=params(WIDE),
        name="pack",
    )(where, owners, owners.reshape(1, blocks), part_tiles, left_factor[0], right_tiles)
    received = lax.all_to_all(message, "rep", split_axis=0, concat_axis=0, tiled=True)
    outgoing = pl.pallas_call(
        spread_kernel,
        out_shape=jax.ShapeDtypeStruct((shards, TILE, LANES), BF16),
        in_specs=[in_smem(), in_smem(), in_vmem()],
        out_specs=in_vmem(),
        compiler_params=params(),
        name="spread",
    )(where, owner_at, received)
    incoming = lax.all_to_all(outgoing, "shard", split_axis=0, concat_axis=0, tiled=True)
    grad = (
        incoming.reshape(shards, panels, rows, LANES).transpose(1, 0, 2, 3).reshape(panels, width, LANES)
    )
    update_panels, grad_copy = pl.pallas_call(
        lambda *refs: update_kernel(count, *refs),
        out_shape=(
            jax.ShapeDtypeStruct((panels, width, LANES), BF16),
            jax.ShapeDtypeStruct((panels, width, LANES), BF16),
        ),
        in_specs=[in_vmem(), in_vmem()],
        out_specs=(in_vmem(), anywhere()),
        scratch_shapes=[pltpu.SemaphoreType.DMA],
        compiler_params=params(),
        cost_estimate=pl.CostEstimate(flops=4 * width**3, bytes_accessed=8 * width**2, transcendentals=0),
        name="update",
    )(grad, received)
    grads = lax.all_gather(grad_copy, "rep", axis=0, tiled=False)
    returned = lax.all_to_all(
        update_panels.reshape(panels * shards, rows, LANES),
        ("rep", "shard"),
        split_axis=0,
        concat_axis=0,
        tiled=True,
    )
    left_new, right_new, update = pl.pallas_call(
        finish_kernel,
        out_shape=(
            jax.ShapeDtypeStruct(left_stat.shape[1:], BF16),
            jax.ShapeDtypeStruct(right_stat.shape[1:], BF16),
            jax.ShapeDtypeStruct((blocks, rows, LANES), BF16),
        ),
        in_specs=[in_smem(), in_smem(), in_smem(), in_vmem(), anywhere(), anywhere(), anywhere()],
        out_specs=(anywhere(), anywhere(), anywhere()),
        scratch_shapes=[
            VMEM((slots, panels, width, LANES), BF16),
            VMEM((slots, quarter, width), BF16),
            VMEM((slots, quarter, width), BF16),
            VMEM((blocks, rows, LANES), BF16),
            pltpu.SemaphoreType.DMA((slots, 3)),
            pltpu.SemaphoreType.DMA((2 * slots + 1,)),
        ],
        compiler_params=params(WIDE),
        cost_estimate=pl.CostEstimate(
            flops=4 * slots * quarter * width**2, bytes_accessed=16 * slots * quarter * width, transcendentals=0
        ),
        name="finish",
    )(where, source, base, returned, grads, left_stat[0], right_stat[0])
    return left_new[None], right_new[None], update


def solution(mesh):
    return jax.shard_map(
        per_device,
        mesh=mesh,
        in_specs=(
            P("rep", None, "shard", None),
            P(),
            P("shard", None, "rep", None),
            P("shard", None, "rep", None),
            P("shard", None, "rep", None),
            P("shard", None, None, "rep"),
        ),
        out_specs=(
            P("shard", None, "rep", None),
            P("shard", None, "rep", None),
            P(None, "shard", "rep"),
        ),
        check_vma=False,
    )
```

```python
import jax
import jax.numpy as jnp
from jax import lax
from jax.experimental import pallas as pl
from jax.experimental.pallas import tpu as pltpu
from jax.sharding import PartitionSpec as P

VMEM = pltpu.VMEM
SMEM = pltpu.SMEM
LIMIT = 40 * 1024 * 1024
WIDE = 58 * 1024 * 1024
F32 = jnp.float32
BF16 = jnp.bfloat16
LANES = 128
TILE = 16


def params(limit=LIMIT):
    return pltpu.CompilerParams(vmem_limit_bytes=limit)


def in_vmem():
    return pl.BlockSpec(memory_space=VMEM)


def in_smem():
    return pl.BlockSpec(memory_space=SMEM)


def anywhere():
    return pl.BlockSpec(memory_space=pl.ANY)


def pack_kernel(owners_ref, part_ref, left_ref, right_ref, out_ref, plan_ref, source_ref, *rest):
    factor_outs = rest[:-14]
    part, message, left, factors, owners, lanes, place, place_at, plan, source = rest[-14:-4]
    in_sems, right_sems, out_sems, sems = rest[-4:]
    classes, count = out_ref.shape[:2]
    blocks = part_ref.shape[0]
    panels = right_ref.shape[1]
    me, replica = lax.axis_index("shard"), lax.axis_index("rep")
    load_owners = [
        pltpu.make_async_copy(owners_ref, owners, sems.at[0]),
        pltpu.make_async_copy(owners_ref, lanes, sems.at[1]),
    ]
    for load in load_owners:
        load.start()
    load_parts = []
    for c in range(classes):
        chunk = pl.ds(c * count, count)
        load_parts.append(pltpu.make_async_copy(part_ref.at[chunk], part.at[chunk], in_sems.at[c]))
        load_parts[c].start()
    load_left = pltpu.make_async_copy(left_ref, left, in_sems.at[classes])
    load_left.start()
    for load in load_owners:
        load.wait()
    owner = lanes[...]
    key = owner * blocks + lax.broadcasted_iota(jnp.int32, owner.shape, 1)

    def compare(b, carry):
        before, base = carry
        other = owners[0, b]
        before = before + jnp.where(key > other * blocks + b, 1, 0)
        return before, base + jnp.where(other < me, 1, 0)

    rank, base = lax.fori_loop(0, blocks, compare, (jnp.zeros_like(key), jnp.int32(0)), unroll=8)
    base = lax.rem(base, classes)
    plan[0, blocks] = base
    cls = lax.rem(rank, classes)
    place[...] = cls * count + lax.div(rank, classes)
    bring = pltpu.make_async_copy(place, place_at, sems.at[2])
    bring.start()
    slots, load_rights = [], []
    for d in range(classes):
        slots.append(lax.rem(lax.rem(replica + d, classes) + classes - base, classes))
        load_rights.append(
            pltpu.make_async_copy(right_ref.at[slots[d]], factors.at[d, pl.ds(panels, panels)], right_sems.at[d])
        )
        load_rights[d].start()
    source[...] = cls * lax.axis_size("shard") + owner
    stores = [pltpu.make_async_copy(source, source_ref, sems.at[3])]
    stores[0].start()
    load_left.wait()
    for d, factor_out in enumerate(factor_outs):
        for h in range(panels):
            factors[d, h] = left[slots[d], :, h * LANES : (h + 1) * LANES]
        load_rights[d].wait()
        stores.append(pltpu.make_async_copy(factors.at[d], factor_out, out_sems.at[classes + d]))
        stores[-1].start()
    bring.wait()
    for load in load_parts:
        load.wait()

    def move(b, _):
        at = place_at[0, b]
        message[at] = part[b]
        plan[0, at] = owners[0, b]
        return 0

    lax.fori_loop(0, blocks, move, 0, unroll=8)
    stores.append(pltpu.make_async_copy(plan, plan_ref, sems.at[4]))
    stores[-1].start()
    for c in range(classes):
        stores.append(pltpu.make_async_copy(message.at[pl.ds(c * count, count)], out_ref.at[c], out_sems.at[c]))
        stores[-1].start()
    for store in stores:
        store.wait()


def spread_kernel(plan_ref, in_ref, out_ref, spread, plan, sems, sem):
    load = pltpu.make_async_copy(plan_ref, plan, sem)
    load.start()
    spread[...] = jnp.zeros_like(spread)
    classes, count = in_ref.shape[:2]
    first = lax.axis_index("rep") * count
    load.wait()

    def add(j, _):
        total = in_ref[0, j].astype(F32)
        for r in range(1, classes):
            total = total + in_ref[r, j].astype(F32)
        spread[plan[0, first + j]] = total.astype(spread.dtype)
        return 0

    lax.fori_loop(0, count, add, 0, unroll=8)
    parts = sems.shape[0]
    length = spread.shape[0] // parts
    stores = []
    for n in range(parts):
        chunk = pl.ds(n * length, length)
        stores.append(pltpu.make_async_copy(spread.at[chunk], out_ref.at[chunk], sems.at[n]))
        stores[n].start()
    for store in stores:
        store.wait()


def update_kernel(grad_ref, *rest):
    factor_refs = rest[:-4]
    out_ref, product, held, sems = rest[-4:]
    panels, width, _ = grad_ref.shape
    rows = width // panels
    replica = lax.axis_index("rep")
    sources = [lax.rem(replica + panels - d, panels) for d in range(panels)]
    grad = jnp.concatenate([grad_ref[c] for c in range(panels)], axis=1)
    for d, factor_ref in enumerate(factor_refs):
        left = jnp.concatenate([factor_ref[h] for h in range(panels)], axis=1)
        product[d * rows : (d + 1) * rows] = jnp.dot(left, grad, preferred_element_type=F32).astype(BF16)
    stores = []
    for d, factor_ref in enumerate(factor_refs):
        right = jnp.concatenate([factor_ref[panels + h] for h in range(panels)], axis=0)
        result = jnp.dot(product[...], right, preferred_element_type=F32).astype(BF16)
        for e in range(panels):
            held[d, e] = result[e * rows : (e + 1) * rows]
        for e in range(panels):
            to = pl.ds(pl.multiple_of(sources[e] * rows, rows), rows)
            stores.append(pltpu.make_async_copy(held.at[d, e], out_ref.at[sources[d], to], sems.at[d, e]))
            stores[-1].start()
    for store in stores:
        store.wait()


def products_kernel(grad_ref, *out_refs):
    panels, width, _ = grad_ref.shape
    rows = width // panels
    replica = lax.axis_index("rep")
    grad = jnp.concatenate([grad_ref[c] for c in range(panels)], axis=1)
    for d, out_ref in enumerate(out_refs):
        to = lax.rem(replica + d, panels)
        start = pl.multiple_of(to * rows, rows)
        own_rows = jnp.concatenate([grad_ref[c, pl.ds(start, rows), :] for c in range(panels)], axis=1)
        left = lax.dot_general(own_rows, grad, (((1,), (1,)), ((), ())), preferred_element_type=F32)
        right = lax.dot_general(grad_ref[to], grad, (((0,), (0,)), ((), ())), preferred_element_type=F32)
        out_ref[0] = left.astype(out_ref.dtype)
        out_ref[1] = right.astype(out_ref.dtype)


def finish_kernel(plan_ref, source_ref, in_ref, left_ref, right_ref, *rest):
    product_refs = rest[:-10]
    left_out, right_out, update_out, lefts, rights, update, plan, source, sems, in_sems = rest[-10:]
    slots = left_ref.shape[0]
    blocks = update.shape[0]
    replica = lax.axis_index("rep")
    load_plan = pltpu.make_async_copy(plan_ref, plan, in_sems.at[0])
    load_source = pltpu.make_async_copy(source_ref, source, in_sems.at[1])
    load_plan.start()
    load_source.start()
    load_plan.wait()
    load_source.wait()
    base = plan[0, blocks]

    def move(b, _):
        update[b] = in_ref[source[0, b]]
        return 0

    lax.fori_loop(0, blocks, move, 0, unroll=8)
    stores = [pltpu.make_async_copy(update, update_out, sems.at[0])]
    stores[0].start()
    for d, product_ref in enumerate(product_refs):
        k = lax.rem(lax.rem(replica + slots - d, slots) + slots - base, slots)
        for n, (old, new, out) in enumerate(((left_ref, lefts, left_out), (right_ref, rights, right_out))):
            new[d] = (0.9 * old[k].astype(F32) + 0.1 * product_ref[n].astype(F32)).astype(new.dtype)
            stores.append(pltpu.make_async_copy(new.at[d], out.at[k], sems.at[len(stores)]))
            stores[-1].start()
    for store in stores:
        store.wait()


def to_others(messages):
    count = len(messages)
    sent = list(messages)
    for d in sorted(range(1, count), key=lambda d: -min(d, count - d)):
        sent[d] = lax.ppermute(messages[d], "rep", [(s, (s + d) % count) for s in range(count)])
    return sent


def per_device(partials, owners, left_stat, right_stat, left_factor, right_factor):
    shards = lax.axis_size("shard")
    classes = lax.axis_size("rep")
    _, blocks, rows, width = partials.shape
    slots = left_stat.shape[1]
    quarter = width // classes
    panels = width // LANES
    count = blocks // classes
    tall = width // TILE

    part_tiles = (
        partials[0].reshape(blocks, rows, panels, LANES).transpose(0, 2, 1, 3).reshape(blocks, TILE, LANES)
    )
    right_tiles = right_factor[0].reshape(slots, panels, LANES, LANES)
    factor_message = jax.ShapeDtypeStruct((2 * panels, LANES, LANES), BF16)
    message, plan, source, *factors = pl.pallas_call(
        pack_kernel,
        out_shape=(
            jax.ShapeDtypeStruct((classes, count, TILE, LANES), BF16),
            jax.ShapeDtypeStruct((1, 2 * LANES), jnp.int32),
            jax.ShapeDtypeStruct((1, blocks), jnp.int32),
            *[factor_message] * classes,
        ),
        in_specs=[anywhere()] * 4,
        out_specs=[anywhere()] * (3 + classes),
        scratch_shapes=[
            VMEM((blocks, TILE, LANES), BF16),
            VMEM((blocks, TILE, LANES), BF16),
            VMEM((slots, quarter, width), BF16),
            VMEM((classes, 2 * panels, LANES, LANES), BF16),
            SMEM((1, blocks), jnp.int32),
            VMEM((1, blocks), jnp.int32),
            VMEM((1, blocks), jnp.int32),
            SMEM((1, blocks), jnp.int32),
            SMEM((1, 2 * LANES), jnp.int32),
            VMEM((1, blocks), jnp.int32),
            pltpu.SemaphoreType.DMA((classes + 1,)),
            pltpu.SemaphoreType.DMA((classes,)),
            pltpu.SemaphoreType.DMA((2 * classes,)),
            pltpu.SemaphoreType.DMA((5,)),
        ],
        compiler_params=params(WIDE),
        name="pack",
    )(owners.reshape(1, blocks), part_tiles, left_factor[0], right_tiles)
    received = lax.all_to_all(message, "rep", split_axis=0, concat_axis=0, tiled=True)
    factors = to_others(factors)
    outgoing = pl.pallas_call(
        spread_kernel,
        out_shape=jax.ShapeDtypeStruct((shards, TILE, LANES), BF16),
        in_specs=[anywhere(), in_vmem()],
        out_specs=anywhere(),
        scratch_shapes=[
            VMEM((shards, TILE, LANES), BF16),
            SMEM((1, 2 * LANES), jnp.int32),
            pltpu.SemaphoreType.DMA((4,)),
            pltpu.SemaphoreType.DMA,
        ],
        compiler_params=params(),
        name="spread",
    )(plan, received)
    incoming = lax.all_to_all(outgoing, "shard", split_axis=0, concat_axis=0, tiled=True)
    grad = (
        incoming.reshape(shards, panels, rows, LANES).transpose(1, 0, 2, 3).reshape(panels, width, LANES)
    )
    update_panels = pl.pallas_call(
        update_kernel,
        out_shape=jax.ShapeDtypeStruct((panels, width, LANES), BF16),
        in_specs=[in_vmem()] * (1 + classes),
        out_specs=anywhere(),
        scratch_shapes=[
            VMEM((width, width), BF16),
            VMEM((panels, panels, quarter, LANES), BF16),
            pltpu.SemaphoreType.DMA((panels, panels)),
        ],
        compiler_params=params(),
        cost_estimate=pl.CostEstimate(flops=4 * width**3, bytes_accessed=8 * width**2, transcendentals=0),
        name="update",
    )(grad, *factors)
    products = pl.pallas_call(
        products_kernel,
        out_shape=[jax.ShapeDtypeStruct((2, quarter, width), BF16)] * classes,
        in_specs=[in_vmem()],
        out_specs=[in_vmem()] * classes,
        compiler_params=params(),
        cost_estimate=pl.CostEstimate(flops=4 * width**3, bytes_accessed=6 * width**2, transcendentals=0),
        name="products",
    )(grad)
    returned = lax.all_to_all(
        update_panels.reshape(panels * shards, rows, LANES),
        ("rep", "shard"),
        split_axis=0,
        concat_axis=0,
        tiled=True,
    )
    products = to_others(products)
    left_new, right_new, update = pl.pallas_call(
        finish_kernel,
        out_shape=(
            jax.ShapeDtypeStruct(left_stat.shape[1:], BF16),
            jax.ShapeDtypeStruct(right_stat.shape[1:], BF16),
            jax.ShapeDtypeStruct((blocks, rows, LANES), BF16),
        ),
        in_specs=[anywhere()] * 2 + [in_vmem()] * (3 + classes),
        out_specs=(anywhere(), anywhere(), anywhere()),
        scratch_shapes=[
            VMEM((slots, quarter, width), BF16),
            VMEM((slots, quarter, width), BF16),
            VMEM((blocks, rows, LANES), BF16),
            SMEM((1, 2 * LANES), jnp.int32),
            SMEM((1, blocks), jnp.int32),
            pltpu.SemaphoreType.DMA((2 * slots + 1,)),
            pltpu.SemaphoreType.DMA((2,)),
        ],
        compiler_params=params(),
        cost_estimate=pl.CostEstimate(
            flops=8 * slots * quarter * width, bytes_accessed=16 * slots * quarter * width, transcendentals=0
        ),
        name="finish",
    )(plan, source, returned, left_stat[0], right_stat[0], *products)
    return left_new[None], right_new[None], update


def solution(mesh):
    return jax.shard_map(
        per_device,
        mesh=mesh,
        in_specs=(
            P("rep", None, "shard", None),
            P(),
            P("shard", None, "rep", None),
            P("shard", None, "rep", None),
            P("shard", None, "rep", None),
            P("shard", None, None, "rep"),
        ),
        out_specs=(
            P("shard", None, "rep", None),
            P("shard", None, "rep", None),
            P(None, "shard", "rep"),
        ),
        check_vma=False,
    )
```

```python
import jax
import jax.numpy as jnp
from jax import lax
from jax.experimental import pallas as pl
from jax.experimental.pallas import tpu as pltpu
from jax.sharding import PartitionSpec as P

VMEM = pltpu.VMEM
SMEM = pltpu.SMEM
LIMIT = 40 * 1024 * 1024
WIDE = 58 * 1024 * 1024
F32 = jnp.float32
BF16 = jnp.bfloat16
LANES = 128
TILE = 16
PLACES = 256
OFFSETS = (2, 3, 1, 0)


def params(limit=LIMIT):
    return pltpu.CompilerParams(vmem_limit_bytes=limit)


def in_vmem():
    return pl.BlockSpec(memory_space=VMEM)


def in_smem():
    return pl.BlockSpec(memory_space=SMEM)


def anywhere():
    return pl.BlockSpec(memory_space=pl.ANY)


def in_hbm():
    return pl.BlockSpec(memory_space=pltpu.HBM)


def pack_kernel(owners_ref, part_ref, left_ref, right_ref, out_ref, plan_ref, *rest):
    factor_outs = rest[:-14]
    part, message, left, factors, owners, lanes, place, place_at, plan, source = rest[-14:-4]
    in_sems, right_sems, out_sems, sems = rest[-4:]
    classes, count = out_ref.shape[:2]
    blocks = part_ref.shape[0]
    panels = right_ref.shape[1]
    me, replica = lax.axis_index("shard"), lax.axis_index("rep")
    load_owners = [
        pltpu.make_async_copy(owners_ref, owners, sems.at[0]),
        pltpu.make_async_copy(owners_ref, lanes, sems.at[1]),
    ]
    for load in load_owners:
        load.start()
    load_parts = []
    for c in range(classes):
        chunk = pl.ds(c * count, count)
        load_parts.append(pltpu.make_async_copy(part_ref.at[chunk], part.at[chunk], in_sems.at[c]))
        load_parts[c].start()
    load_left = pltpu.make_async_copy(left_ref, left, in_sems.at[classes])
    load_left.start()
    for load in load_owners:
        load.wait()
    owner = lanes[...]
    key = owner * blocks + lax.broadcasted_iota(jnp.int32, owner.shape, 1)

    def compare(b, carry):
        before, base = carry
        other = owners[0, b]
        before = before + jnp.where(key > other * blocks + b, 1, 0)
        return before, base + jnp.where(other < me, 1, 0)

    rank, base = lax.fori_loop(0, blocks, compare, (jnp.zeros_like(key), jnp.int32(0)), unroll=8)
    base = lax.rem(base, classes)
    plan[0, blocks] = base
    cls = lax.rem(rank, classes)
    place[...] = cls * count + lax.div(rank, classes)
    bring = pltpu.make_async_copy(place, place_at, sems.at[2])
    bring.start()
    slots, load_rights = [], []
    for n, d in enumerate(OFFSETS):
        slots.append(lax.rem(lax.rem(replica + d, classes) + classes - base, classes))
        load_rights.append(
            pltpu.make_async_copy(right_ref.at[slots[n]], factors.at[n, pl.ds(panels, panels)], right_sems.at[n])
        )
        load_rights[n].start()
    source[:, pl.ds(0, blocks)] = cls * lax.axis_size("shard") + owner
    stores = [pltpu.make_async_copy(source, plan_ref.at[:, pl.ds(PLACES, PLACES)], sems.at[3])]
    stores[0].start()
    load_left.wait()
    for d, factor_out in enumerate(factor_outs):
        for h in range(panels):
            factors[d, h] = left[slots[d], :, h * LANES : (h + 1) * LANES]
        load_rights[d].wait()
        stores.append(pltpu.make_async_copy(factors.at[d], factor_out, out_sems.at[classes + d]))
        stores[-1].start()
    bring.wait()
    for load in load_parts:
        load.wait()

    def move(b, _):
        at = place_at[0, b]
        message[at] = part[b]
        plan[0, at] = owners[0, b]
        return 0

    lax.fori_loop(0, blocks, move, 0, unroll=8)
    stores.append(pltpu.make_async_copy(plan, plan_ref.at[:, pl.ds(0, PLACES)], sems.at[4]))
    stores[-1].start()
    for c in range(classes):
        stores.append(pltpu.make_async_copy(message.at[pl.ds(c * count, count)], out_ref.at[c], out_sems.at[c]))
        stores[-1].start()
    for store in stores:
        store.wait()


def spread_kernel(plan_ref, in_ref, out_ref, spread, plan, sems, sem):
    load = pltpu.make_async_copy(plan_ref.at[:, pl.ds(0, PLACES)], plan, sem)
    load.start()
    spread[...] = jnp.zeros_like(spread)
    classes, count = in_ref.shape[:2]
    first = lax.axis_index("rep") * count
    load.wait()

    def add(j, _):
        total = in_ref[0, j].astype(F32)
        for r in range(1, classes):
            total = total + in_ref[r, j].astype(F32)
        spread[plan[0, first + j]] = total.astype(spread.dtype)
        return 0

    lax.fori_loop(0, count, add, 0, unroll=8)
    parts = sems.shape[0]
    length = spread.shape[0] // parts
    stores = []
    for n in range(parts):
        chunk = pl.ds(n * length, length)
        stores.append(pltpu.make_async_copy(spread.at[chunk], out_ref.at[chunk], sems.at[n]))
        stores[n].start()
    for store in stores:
        store.wait()


def update_kernel(grad_ref, after_ref, *rest):
    del after_ref
    factor_refs = rest[:-4]
    out_ref, product, held, sems = rest[-4:]
    panels, width, _ = grad_ref.shape
    rows = width // panels
    replica = lax.axis_index("rep")
    sources = [lax.rem(replica + panels - d, panels) for d in OFFSETS]
    grad = jnp.concatenate([grad_ref[c] for c in range(panels)], axis=1)
    for d, factor_ref in enumerate(factor_refs):
        left = jnp.concatenate([factor_ref[h] for h in range(panels)], axis=1)
        product[d * rows : (d + 1) * rows] = jnp.dot(left, grad, preferred_element_type=F32).astype(BF16)
    stores = []
    for d, factor_ref in enumerate(factor_refs):
        right = jnp.concatenate([factor_ref[panels + h] for h in range(panels)], axis=0)
        result = jnp.dot(product[...], right, preferred_element_type=F32).astype(BF16)
        for e in range(panels):
            held[d, e] = result[e * rows : (e + 1) * rows]
        for e in range(panels):
            to = pl.ds(pl.multiple_of(sources[e] * rows, rows), rows)
            stores.append(pltpu.make_async_copy(held.at[d, e], out_ref.at[sources[d], to], sems.at[d, e]))
            stores[-1].start()
    for store in stores:
        store.wait()


def products_kernel(grad_ref, *out_refs):
    panels, width, _ = grad_ref.shape
    rows = width // panels
    replica = lax.axis_index("rep")
    grad = jnp.concatenate([grad_ref[c] for c in range(panels)], axis=1)
    for d, out_ref in zip(OFFSETS, out_refs, strict=True):
        to = lax.rem(replica + d, panels)
        start = pl.multiple_of(to * rows, rows)
        own_rows = jnp.concatenate([grad_ref[c, pl.ds(start, rows), :] for c in range(panels)], axis=1)
        left = lax.dot_general(own_rows, grad, (((1,), (1,)), ((), ())), preferred_element_type=F32)
        right = lax.dot_general(grad_ref[to], grad, (((0,), (0,)), ((), ())), preferred_element_type=F32)
        out_ref[0] = left.astype(out_ref.dtype)
        out_ref[1] = right.astype(out_ref.dtype)


def finish_kernel(plan_ref, in_ref, left_ref, right_ref, *rest):
    product_refs = rest[:-9]
    left_out, right_out, update_out, lefts, rights, update, plan, sems, in_sem = rest[-9:]
    slots = left_ref.shape[0]
    blocks = update.shape[0]
    replica = lax.axis_index("rep")
    load = pltpu.make_async_copy(plan_ref.at[:, pl.ds(0, 2 * PLACES)], plan, in_sem)
    load.start()
    load.wait()
    base = plan[0, blocks]

    def move(b, _):
        update[b] = in_ref[plan[0, PLACES + b]]
        return 0

    lax.fori_loop(0, blocks, move, 0, unroll=8)
    stores = [pltpu.make_async_copy(update, update_out, sems.at[0])]
    stores[0].start()
    for i, (d, product_ref) in enumerate(zip(OFFSETS, product_refs, strict=True)):
        k = lax.rem(lax.rem(replica + slots - d, slots) + slots - base, slots)
        for n, (old, new, out) in enumerate(((left_ref, lefts, left_out), (right_ref, rights, right_out))):
            new[i] = (0.9 * old[k].astype(F32) + 0.1 * product_ref[n].astype(F32)).astype(new.dtype)
            stores.append(pltpu.make_async_copy(new.at[i], out.at[k], sems.at[len(stores)]))
            stores[-1].start()
    for store in stores:
        store.wait()


def to_others(messages):
    count = len(messages)
    return [
        lax.ppermute(message, "rep", [(s, (s + d) % count) for s in range(count)]) if d else message
        for message, d in zip(messages, OFFSETS, strict=True)
    ]


def per_device(partials, owners, left_stat, right_stat, left_factor, right_factor):
    shards = lax.axis_size("shard")
    classes = lax.axis_size("rep")
    _, blocks, rows, width = partials.shape
    slots = left_stat.shape[1]
    quarter = width // classes
    panels = width // LANES
    count = blocks // classes
    tall = width // TILE

    part_tiles = (
        partials[0].reshape(blocks, rows, panels, LANES).transpose(0, 2, 1, 3).reshape(blocks, TILE, LANES)
    )
    right_tiles = right_factor[0].reshape(slots, panels, LANES, LANES)
    factor_message = jax.ShapeDtypeStruct((2 * panels, LANES, LANES), BF16)
    message, plan, *factors = pl.pallas_call(
        pack_kernel,
        out_shape=(
            jax.ShapeDtypeStruct((classes, count, TILE, LANES), BF16),
            jax.ShapeDtypeStruct((1, 2 * PLACES), jnp.int32),
            *[factor_message] * classes,
        ),
        in_specs=[anywhere()] * 4,
        out_specs=[anywhere()] * (2 + classes),
        scratch_shapes=[
            VMEM((blocks, TILE, LANES), BF16),
            VMEM((blocks, TILE, LANES), BF16),
            VMEM((slots, quarter, width), BF16),
            VMEM((classes, 2 * panels, LANES, LANES), BF16),
            SMEM((1, blocks), jnp.int32),
            VMEM((1, blocks), jnp.int32),
            VMEM((1, blocks), jnp.int32),
            SMEM((1, blocks), jnp.int32),
            SMEM((1, PLACES), jnp.int32),
            VMEM((1, PLACES), jnp.int32),
            pltpu.SemaphoreType.DMA((classes + 1,)),
            pltpu.SemaphoreType.DMA((classes,)),
            pltpu.SemaphoreType.DMA((2 * classes,)),
            pltpu.SemaphoreType.DMA((5,)),
        ],
        compiler_params=params(WIDE),
        name="pack",
    )(owners.reshape(1, blocks), part_tiles, left_factor[0], right_tiles)
    received = lax.all_to_all(message, "rep", split_axis=0, concat_axis=0, tiled=True)
    factors = to_others(factors)
    outgoing = pl.pallas_call(
        spread_kernel,
        out_shape=jax.ShapeDtypeStruct((shards, TILE, LANES), BF16),
        in_specs=[in_hbm(), in_vmem()],
        out_specs=anywhere(),
        scratch_shapes=[
            VMEM((shards, TILE, LANES), BF16),
            SMEM((1, PLACES), jnp.int32),
            pltpu.SemaphoreType.DMA((4,)),
            pltpu.SemaphoreType.DMA,
        ],
        compiler_params=params(),
        name="spread",
    )(plan, received)
    incoming = lax.all_to_all(outgoing, "shard", split_axis=0, concat_axis=0, tiled=True)
    grad = (
        incoming.reshape(shards, panels, rows, LANES).transpose(1, 0, 2, 3).reshape(panels, width, LANES)
    )
    products = pl.pallas_call(
        products_kernel,
        out_shape=[jax.ShapeDtypeStruct((2, quarter, width), BF16)] * classes,
        in_specs=[in_vmem()],
        out_specs=[in_vmem()] * classes,
        compiler_params=params(),
        cost_estimate=pl.CostEstimate(flops=4 * width**3, bytes_accessed=6 * width**2, transcendentals=0),
        name="products",
    )(grad)
    update_panels = pl.pallas_call(
        update_kernel,
        out_shape=jax.ShapeDtypeStruct((panels, width, LANES), BF16),
        in_specs=[in_vmem(), anywhere()] + [in_vmem()] * classes,
        out_specs=anywhere(),
        scratch_shapes=[
            VMEM((width, width), BF16),
            VMEM((panels, panels, quarter, LANES), BF16),
            pltpu.SemaphoreType.DMA((panels, panels)),
        ],
        compiler_params=params(),
        cost_estimate=pl.CostEstimate(flops=4 * width**3, bytes_accessed=8 * width**2, transcendentals=0),
        name="update",
    )(grad, products[-1], *factors)
    returned = lax.all_to_all(
        update_panels.reshape(panels * shards, rows, LANES),
        ("rep", "shard"),
        split_axis=0,
        concat_axis=0,
        tiled=True,
    )
    products = to_others(products)
    left_new, right_new, update = pl.pallas_call(
        finish_kernel,
        out_shape=(
            jax.ShapeDtypeStruct(left_stat.shape[1:], BF16),
            jax.ShapeDtypeStruct(right_stat.shape[1:], BF16),
            jax.ShapeDtypeStruct((blocks, rows, LANES), BF16),
        ),
        in_specs=[in_hbm()] + [in_vmem()] * (3 + classes),
        out_specs=(anywhere(), anywhere(), anywhere()),
        scratch_shapes=[
            VMEM((slots, quarter, width), BF16),
            VMEM((slots, quarter, width), BF16),
            VMEM((blocks, rows, LANES), BF16),
            SMEM((1, 2 * PLACES), jnp.int32),
            pltpu.SemaphoreType.DMA((2 * slots + 1,)),
            pltpu.SemaphoreType.DMA,
        ],
        compiler_params=params(),
        cost_estimate=pl.CostEstimate(
            flops=8 * slots * quarter * width, bytes_accessed=16 * slots * quarter * width, transcendentals=0
        ),
        name="finish",
    )(plan, returned, left_stat[0], right_stat[0], *products)
    return left_new[None], right_new[None], update


def solution(mesh):
    return jax.shard_map(
        per_device,
        mesh=mesh,
        in_specs=(
            P("rep", None, "shard", None),
            P(),
            P("shard", None, "rep", None),
            P("shard", None, "rep", None),
            P("shard", None, "rep", None),
            P("shard", None, None, "rep"),
        ),
        out_specs=(
            P("shard", None, "rep", None),
            P("shard", None, "rep", None),
            P(None, "shard", "rep"),
        ),
        check_vma=False,
    )
```

```python
import functools

import jax
import jax.numpy as jnp
from jax import lax
from jax.experimental import pallas as pl
from jax.experimental.pallas import tpu as pltpu
from jax.sharding import PartitionSpec as P

VMEM = pltpu.VMEM
SMEM = pltpu.SMEM
LIMIT = 40 * 1024 * 1024
WIDE = 58 * 1024 * 1024
F32 = jnp.float32
BF16 = jnp.bfloat16
LANES = 128
TILE = 16
PLACES = 256
BASE_AT = PLACES - 1
OFFSETS = (2, 3, 1, 0)
HOLD = 1 << 34


def params(limit=LIMIT):
    return pltpu.CompilerParams(vmem_limit_bytes=limit)


def in_vmem():
    return pl.BlockSpec(memory_space=VMEM)


def in_smem():
    return pl.BlockSpec(memory_space=SMEM)


def anywhere():
    return pl.BlockSpec(memory_space=pl.ANY)


def in_hbm():
    return pl.BlockSpec(memory_space=pltpu.HBM)


def pack_kernel(
    owners_ref, part_ref, out_ref, plan_ref,
    part, message, owners, lanes, padded, place, place_at, plan, source, in_sems, out_sems, sems,
):
    classes, count = out_ref.shape[:2]
    blocks = part_ref.shape[0]
    load_owners = [
        pltpu.make_async_copy(owners_ref, owners, sems.at[0]),
        pltpu.make_async_copy(owners_ref, lanes, sems.at[1]),
    ]
    for load in load_owners:
        load.start()
    load_parts = []
    for c in range(classes):
        chunk = pl.ds(c * count, count)
        load_parts.append(pltpu.make_async_copy(part_ref.at[chunk], part.at[chunk], in_sems.at[c]))
        load_parts[c].start()
    for load in load_owners:
        load.wait()
    padded[...] = jnp.full_like(padded, lax.axis_size("shard"))
    padded[:, pl.ds(0, blocks)] = lanes[...]
    owner = padded[...]
    key = owner * PLACES + lax.broadcasted_iota(jnp.int32, owner.shape, 1)
    rank = jnp.zeros_like(key)
    for h in range(PLACES // LANES):
        square = jnp.broadcast_to(key[:, h * LANES : (h + 1) * LANES], (LANES, LANES)).T
        other = jnp.concatenate([square] * (PLACES // LANES), axis=1)
        rank = rank + jnp.sum(jnp.where(other < key, 1, 0), axis=0, keepdims=True)
    cls = lax.rem(rank, classes)
    place[...] = cls * count + lax.div(rank, classes)
    bring = pltpu.make_async_copy(place, place_at, sems.at[2])
    bring.start()
    source[...] = cls * lax.axis_size("shard") + owner
    stores = [pltpu.make_async_copy(source, plan_ref.at[:, pl.ds(PLACES, PLACES)], sems.at[3])]
    stores[0].start()
    base = jnp.sum(jnp.where(owner < lax.axis_index("shard"), 1, 0))
    plan[0, BASE_AT] = lax.rem(base, classes)
    bring.wait()
    for load in load_parts:
        load.wait()

    def move(b, _):
        at = place_at[0, b]
        message[at] = part[b]
        plan[0, at] = owners[0, b]
        return 0

    lax.fori_loop(0, blocks, move, 0, unroll=8)
    stores.append(pltpu.make_async_copy(plan, plan_ref.at[:, pl.ds(0, PLACES)], sems.at[4]))
    stores[-1].start()
    for c in range(classes):
        stores.append(pltpu.make_async_copy(message.at[pl.ds(c * count, count)], out_ref.at[c], out_sems.at[c]))
        stores[-1].start()
    for store in stores:
        store.wait()


def factors_kernel(plan_ref, left_ref, right_ref, *rest):
    factor_outs = rest[:-6]
    left, factors, plan, in_sems, out_sems, sem = rest[-6:]
    classes = len(OFFSETS)
    panels = right_ref.shape[1]
    replica = lax.axis_index("rep")
    load_plan = pltpu.make_async_copy(plan_ref.at[:, pl.ds(0, PLACES)], plan, sem)
    load_plan.start()
    load_left = pltpu.make_async_copy(left_ref, left, in_sems.at[classes])
    load_left.start()
    load_plan.wait()
    slots, loads, stores = [], [], []
    for n, d in enumerate(OFFSETS):
        slots.append(lax.rem(lax.rem(replica + d, classes) + classes - plan[0, BASE_AT], classes))
        loads.append(
            pltpu.make_async_copy(right_ref.at[slots[n]], factors.at[n, pl.ds(panels, panels)], in_sems.at[n])
        )
        loads[n].start()
    load_left.wait()
    for n, factor_out in enumerate(factor_outs):
        for h in range(panels):
            factors[n, h] = left[slots[n], :, h * LANES : (h + 1) * LANES]
        loads[n].wait()
        stores.append(pltpu.make_async_copy(factors.at[n], factor_out, out_sems.at[n]))
        stores[n].start()
    for store in stores:
        store.wait()


def spread_kernel(plan_ref, after_ref, in_ref, out_ref, spread, plan, sems, sem):
    del after_ref
    load = pltpu.make_async_copy(plan_ref.at[:, pl.ds(0, PLACES)], plan, sem)
    load.start()
    spread[...] = jnp.zeros_like(spread)
    classes, count = in_ref.shape[:2]
    first = lax.axis_index("rep") * count
    load.wait()

    def add(j, _):
        total = in_ref[0, j].astype(F32)
        for r in range(1, classes):
            total = total + in_ref[r, j].astype(F32)
        spread[plan[0, first + j]] = total.astype(spread.dtype)
        return 0

    lax.fori_loop(0, count, add, 0, unroll=8)
    parts = sems.shape[0]
    length = spread.shape[0] // parts
    stores = []
    for n in range(parts):
        chunk = pl.ds(n * length, length)
        stores.append(pltpu.make_async_copy(spread.at[chunk], out_ref.at[chunk], sems.at[n]))
        stores[n].start()
    for store in stores:
        store.wait()


def update_kernel(grad_ref, after_ref, *rest):
    del after_ref
    factor_refs = rest[:-3]
    out_ref, held, sems = rest[-3:]
    panels, width, _ = grad_ref.shape
    rows = width // panels
    replica = lax.axis_index("rep")
    sources = [lax.rem(replica + panels - d, panels) for d in OFFSETS]
    grad = jnp.concatenate([grad_ref[c] for c in range(panels)], axis=1)
    right = jnp.concatenate(
        [
            jnp.concatenate([factor_ref[panels + h] for h in range(panels)], axis=0)
            for factor_ref in factor_refs
        ],
        axis=1,
    )
    stores = []
    for i, factor_ref in enumerate(factor_refs):
        left = jnp.concatenate([factor_ref[h] for h in range(panels)], axis=1)
        product = jnp.dot(left, grad, preferred_element_type=F32).astype(BF16)
        result = jnp.dot(product, right, preferred_element_type=F32).astype(BF16)
        to = pl.ds(pl.multiple_of(sources[i] * rows, rows), rows)
        for e in range(panels):
            held[i, e] = result[:, e * LANES : (e + 1) * LANES]
            stores.append(pltpu.make_async_copy(held.at[i, e], out_ref.at[sources[e], to], sems.at[i, e]))
            stores[-1].start()
    for store in stores:
        store.wait()


def products_kernel(offsets, grad_ref, *out_refs):
    panels, width, _ = grad_ref.shape
    rows = width // panels
    replica = lax.axis_index("rep")
    grad = jnp.concatenate([grad_ref[c] for c in range(panels)], axis=1)
    for d, out_ref in zip(offsets, out_refs, strict=True):
        to = lax.rem(replica + d, panels)
        start = pl.multiple_of(to * rows, rows)
        own_rows = jnp.concatenate([grad_ref[c, pl.ds(start, rows), :] for c in range(panels)], axis=1)
        left = lax.dot_general(own_rows, grad, (((1,), (1,)), ((), ())), preferred_element_type=F32)
        right = lax.dot_general(grad_ref[to], grad, (((0,), (0,)), ((), ())), preferred_element_type=F32)
        out_ref[0] = left.astype(out_ref.dtype)
        out_ref[1] = right.astype(out_ref.dtype)


def hold_kernel(in_ref, out_ref):
    out_ref[...] = in_ref[...]


def stats_kernel(plan_ref, left_ref, right_ref, *rest):
    product_refs = rest[:-7]
    left_out, right_out, lefts, rights, plan, sems, in_sem = rest[-7:]
    slots = left_ref.shape[0]
    replica = lax.axis_index("rep")
    load = pltpu.make_async_copy(plan_ref.at[:, pl.ds(0, PLACES)], plan, in_sem)
    load.start()
    load.wait()
    base = plan[0, BASE_AT]
    stores = []
    for i, (d, product_ref) in enumerate(zip(OFFSETS, product_refs, strict=True)):
        k = lax.rem(lax.rem(replica + slots - d, slots) + slots - base, slots)
        for n, (old, new, out) in enumerate(((left_ref, lefts, left_out), (right_ref, rights, right_out))):
            new[i] = (0.9 * old[k].astype(F32) + 0.1 * product_ref[n].astype(F32)).astype(new.dtype)
            stores.append(pltpu.make_async_copy(new.at[i], out.at[k], sems.at[len(stores)]))
            stores[-1].start()
    for store in stores:
        store.wait()


def collect_kernel(plan_ref, in_ref, out_ref, update, plan, sem, in_sem):
    load = pltpu.make_async_copy(plan_ref.at[:, pl.ds(PLACES, PLACES)], plan, in_sem)
    load.start()
    load.wait()

    def move(b, _):
        update[b] = in_ref[plan[0, b]]
        return 0

    lax.fori_loop(0, update.shape[0], move, 0, unroll=8)
    store = pltpu.make_async_copy(update, out_ref, sem)
    store.start()
    store.wait()


def to_others(messages):
    count = len(messages)
    return [
        lax.ppermute(message, "rep", [(s, (s + d) % count) for s in range(count)]) if d else message
        for message, d in zip(messages, OFFSETS, strict=True)
    ]


def per_device(partials, owners, left_stat, right_stat, left_factor, right_factor):
    shards = lax.axis_size("shard")
    classes = lax.axis_size("rep")
    _, blocks, rows, width = partials.shape
    slots = left_stat.shape[1]
    quarter = width // classes
    panels = width // LANES
    count = blocks // classes
    tall = width // TILE

    part_tiles = (
        partials[0].reshape(blocks, rows, panels, LANES).transpose(0, 2, 1, 3).reshape(blocks, TILE, LANES)
    )
    right_tiles = right_factor[0].reshape(slots, panels, LANES, LANES)
    factor_message = jax.ShapeDtypeStruct((2 * panels, LANES, LANES), BF16)
    message, plan = pl.pallas_call(
        pack_kernel,
        out_shape=(
            jax.ShapeDtypeStruct((classes, count, TILE, LANES), BF16),
            jax.ShapeDtypeStruct((1, 2 * PLACES), jnp.int32),
        ),
        in_specs=[anywhere()] * 2,
        out_specs=[anywhere()] * 2,
        scratch_shapes=[
            VMEM((blocks, TILE, LANES), BF16),
            VMEM((blocks, TILE, LANES), BF16),
            SMEM((1, blocks), jnp.int32),
            VMEM((1, blocks), jnp.int32),
            VMEM((1, PLACES), jnp.int32),
            VMEM((1, PLACES), jnp.int32),
            SMEM((1, PLACES), jnp.int32),
            SMEM((1, PLACES), jnp.int32),
            VMEM((1, PLACES), jnp.int32),
            pltpu.SemaphoreType.DMA((classes,)),
            pltpu.SemaphoreType.DMA((classes,)),
            pltpu.SemaphoreType.DMA((5,)),
        ],
        compiler_params=params(WIDE),
        name="pack",
    )(owners.reshape(1, blocks), part_tiles)
    received = lax.all_to_all(message, "rep", split_axis=0, concat_axis=0, tiled=True)
    factors = pl.pallas_call(
        factors_kernel,
        out_shape=[factor_message] * classes,
        in_specs=[in_hbm(), anywhere(), anywhere()],
        out_specs=[anywhere()] * classes,
        scratch_shapes=[
            VMEM((slots, quarter, width), BF16),
            VMEM((classes, 2 * panels, LANES, LANES), BF16),
            SMEM((1, PLACES), jnp.int32),
            pltpu.SemaphoreType.DMA((classes + 1,)),
            pltpu.SemaphoreType.DMA((classes,)),
            pltpu.SemaphoreType.DMA,
        ],
        compiler_params=params(),
        cost_estimate=pl.CostEstimate(flops=0, bytes_accessed=8 * width**2, transcendentals=0),
        name="factors",
    )(plan, left_factor[0], right_tiles)
    packed = factors[-1]
    factors = to_others(factors)
    outgoing = pl.pallas_call(
        spread_kernel,
        out_shape=jax.ShapeDtypeStruct((shards, TILE, LANES), BF16),
        in_specs=[in_hbm(), in_hbm(), in_vmem()],
        out_specs=anywhere(),
        scratch_shapes=[
            VMEM((shards, TILE, LANES), BF16),
            SMEM((1, PLACES), jnp.int32),
            pltpu.SemaphoreType.DMA((4,)),
            pltpu.SemaphoreType.DMA,
        ],
        compiler_params=params(),
        name="spread",
    )(plan, packed, received)
    incoming = lax.all_to_all(outgoing, "shard", split_axis=0, concat_axis=0, tiled=True)
    grad = (
        incoming.reshape(shards, panels, rows, LANES).transpose(1, 0, 2, 3).reshape(panels, width, LANES)
    )
    products = []
    for offsets in (OFFSETS[:1], OFFSETS[1:]):
        products += pl.pallas_call(
            functools.partial(products_kernel, offsets),
            out_shape=[jax.ShapeDtypeStruct((2, quarter, width), BF16)] * len(offsets),
            in_specs=[in_vmem()],
            out_specs=[in_vmem()] * len(offsets),
            compiler_params=params(),
            cost_estimate=pl.CostEstimate(
                flops=len(offsets) * width**3, bytes_accessed=2 * width**2, transcendentals=0
            ),
            name="products",
        )(grad)
    update_panels = pl.pallas_call(
        update_kernel,
        out_shape=jax.ShapeDtypeStruct((panels, width, LANES), BF16),
        in_specs=[in_vmem(), anywhere()] + [in_vmem()] * classes,
        out_specs=anywhere(),
        scratch_shapes=[
            VMEM((panels, panels, quarter, LANES), BF16),
            pltpu.SemaphoreType.DMA((panels, panels)),
        ],
        compiler_params=params(),
        cost_estimate=pl.CostEstimate(flops=4 * width**3, bytes_accessed=8 * width**2, transcendentals=0),
        name="update",
    )(grad, products[0], *factors)
    returned = lax.all_to_all(
        update_panels.reshape(panels * shards, rows, LANES),
        ("rep", "shard"),
        split_axis=0,
        concat_axis=0,
        tiled=True,
    )
    products = to_others(products)
    products[0] = pl.pallas_call(
        hold_kernel,
        out_shape=jax.ShapeDtypeStruct((2, quarter, width), BF16),
        in_specs=[in_vmem()],
        out_specs=in_vmem(),
        compiler_params=params(),
        cost_estimate=pl.CostEstimate(flops=HOLD, bytes_accessed=8 * quarter * width, transcendentals=0),
        name="hold",
    )(products[0])
    left_new, right_new = pl.pallas_call(
        stats_kernel,
        out_shape=(
            jax.ShapeDtypeStruct(left_stat.shape[1:], BF16),
            jax.ShapeDtypeStruct(right_stat.shape[1:], BF16),
        ),
        in_specs=[in_hbm()] + [in_vmem()] * (2 + classes),
        out_specs=(anywhere(), anywhere()),
        scratch_shapes=[
            VMEM((slots, quarter, width), BF16),
            VMEM((slots, quarter, width), BF16),
            SMEM((1, PLACES), jnp.int32),
            pltpu.SemaphoreType.DMA((2 * slots,)),
            pltpu.SemaphoreType.DMA,
        ],
        compiler_params=params(),
        cost_estimate=pl.CostEstimate(
            flops=8 * slots * quarter * width, bytes_accessed=12 * slots * quarter * width, transcendentals=0
        ),
        name="stats",
    )(plan, left_stat[0], right_stat[0], *products)
    update = pl.pallas_call(
        collect_kernel,
        out_shape=jax.ShapeDtypeStruct((blocks, rows, LANES), BF16),
        in_specs=[in_hbm(), in_vmem()],
        out_specs=anywhere(),
        scratch_shapes=[
            VMEM((blocks, rows, LANES), BF16),
            SMEM((1, PLACES), jnp.int32),
            pltpu.SemaphoreType.DMA,
            pltpu.SemaphoreType.DMA,
        ],
        compiler_params=params(),
        cost_estimate=pl.CostEstimate(flops=0, bytes_accessed=4 * blocks * rows * LANES, transcendentals=0),
        name="collect",
    )(plan, returned)
    return left_new[None], right_new[None], update


def solution(mesh):
    return jax.shard_map(
        per_device,
        mesh=mesh,
        in_specs=(
            P("rep", None, "shard", None),
            P(),
            P("shard", None, "rep", None),
            P("shard", None, "rep", None),
            P("shard", None, "rep", None),
            P("shard", None, None, "rep"),
        ),
        out_specs=(
            P("shard", None, "rep", None),
            P("shard", None, "rep", None),
            P(None, "shard", "rep"),
        ),
        check_vma=False,
    )
```

```python
import functools

import jax
import jax.numpy as jnp
from jax import lax
from jax.experimental import pallas as pl
from jax.experimental.pallas import tpu as pltpu
from jax.sharding import PartitionSpec as P

VMEM = pltpu.VMEM
SMEM = pltpu.SMEM
LIMIT = 40 * 1024 * 1024
WIDE = 58 * 1024 * 1024
F32 = jnp.float32
BF16 = jnp.bfloat16
LANES = 128
TILE = 16
PLACES = 256
BASE_AT = PLACES - 1
OFFSETS = (2, 1, 3, 0)
HOLD = 1 << 34


def params(limit=LIMIT):
    return pltpu.CompilerParams(vmem_limit_bytes=limit)


def in_vmem():
    return pl.BlockSpec(memory_space=VMEM)


def in_smem():
    return pl.BlockSpec(memory_space=SMEM)


def anywhere():
    return pl.BlockSpec(memory_space=pl.ANY)


def in_hbm():
    return pl.BlockSpec(memory_space=pltpu.HBM)


def pack_kernel(
    owners_ref, part_ref, out_ref, plan_ref,
    part, message, owners, lanes, padded, place, place_at, plan, source, in_sems, out_sems, sems,
):
    classes, count = out_ref.shape[:2]
    blocks = part_ref.shape[0]
    load_owners = [
        pltpu.make_async_copy(owners_ref, owners, sems.at[0]),
        pltpu.make_async_copy(owners_ref, lanes, sems.at[1]),
    ]
    for load in load_owners:
        load.start()
    load_parts = []
    for c in range(classes):
        chunk = pl.ds(c * count, count)
        load_parts.append(pltpu.make_async_copy(part_ref.at[chunk], part.at[chunk], in_sems.at[c]))
        load_parts[c].start()
    for load in load_owners:
        load.wait()
    padded[...] = jnp.full_like(padded, lax.axis_size("shard"))
    padded[:, pl.ds(0, blocks)] = lanes[...]
    owner = padded[...]
    key = owner * PLACES + lax.broadcasted_iota(jnp.int32, owner.shape, 1)
    rank = jnp.zeros_like(key)
    for h in range(PLACES // LANES):
        square = jnp.broadcast_to(key[:, h * LANES : (h + 1) * LANES], (LANES, LANES)).T
        other = jnp.concatenate([square] * (PLACES // LANES), axis=1)
        rank = rank + jnp.sum(jnp.where(other < key, 1, 0), axis=0, keepdims=True)
    cls = lax.rem(rank, classes)
    place[...] = cls * count + lax.div(rank, classes)
    bring = pltpu.make_async_copy(place, place_at, sems.at[2])
    bring.start()
    source[...] = cls * lax.axis_size("shard") + owner
    stores = [pltpu.make_async_copy(source, plan_ref.at[:, pl.ds(PLACES, PLACES)], sems.at[3])]
    stores[0].start()
    base = jnp.sum(jnp.where(owner < lax.axis_index("shard"), 1, 0))
    plan[0, BASE_AT] = lax.rem(base, classes)
    bring.wait()
    for load in load_parts:
        load.wait()

    def move(b, _):
        at = place_at[0, b]
        message[at] = part[b]
        plan[0, at] = owners[0, b]
        return 0

    lax.fori_loop(0, blocks, move, 0, unroll=8)
    stores.append(pltpu.make_async_copy(plan, plan_ref.at[:, pl.ds(0, PLACES)], sems.at[4]))
    stores[-1].start()
    for c in range(classes):
        stores.append(pltpu.make_async_copy(message.at[pl.ds(c * count, count)], out_ref.at[c], out_sems.at[c]))
        stores[-1].start()
    for store in stores:
        store.wait()


def factors_kernel(plan_ref, left_ref, right_ref, *rest):
    factor_outs = rest[:-6]
    left, factors, plan, in_sems, out_sems, sem = rest[-6:]
    classes = len(OFFSETS)
    panels = right_ref.shape[1]
    replica = lax.axis_index("rep")
    load_plan = pltpu.make_async_copy(plan_ref.at[:, pl.ds(0, PLACES)], plan, sem)
    load_plan.start()
    load_left = pltpu.make_async_copy(left_ref, left, in_sems.at[classes])
    load_left.start()
    load_plan.wait()
    slots, loads, stores = [], [], []
    for n, d in enumerate(OFFSETS):
        slots.append(lax.rem(lax.rem(replica + d, classes) + classes - plan[0, BASE_AT], classes))
        loads.append(
            pltpu.make_async_copy(right_ref.at[slots[n]], factors.at[n, pl.ds(panels, panels)], in_sems.at[n])
        )
        loads[n].start()
    load_left.wait()
    for n, factor_out in enumerate(factor_outs):
        for h in range(panels):
            factors[n, h] = left[slots[n], :, h * LANES : (h + 1) * LANES]
        loads[n].wait()
        stores.append(pltpu.make_async_copy(factors.at[n], factor_out, out_sems.at[n]))
        stores[n].start()
    for store in stores:
        store.wait()


def spread_kernel(plan_ref, after_ref, in_ref, out_ref, spread, plan, sems, sem):
    del after_ref
    load = pltpu.make_async_copy(plan_ref.at[:, pl.ds(0, PLACES)], plan, sem)
    load.start()
    spread[...] = jnp.zeros_like(spread)
    classes, count = in_ref.shape[:2]
    first = lax.axis_index("rep") * count
    load.wait()

    def add(j, _):
        total = in_ref[0, j].astype(F32)
        for r in range(1, classes):
            total = total + in_ref[r, j].astype(F32)
        spread[plan[0, first + j]] = total.astype(spread.dtype)
        return 0

    lax.fori_loop(0, count, add, 0, unroll=8)
    parts = sems.shape[0]
    length = spread.shape[0] // parts
    stores = []
    for n in range(parts):
        chunk = pl.ds(n * length, length)
        stores.append(pltpu.make_async_copy(spread.at[chunk], out_ref.at[chunk], sems.at[n]))
        stores[n].start()
    for store in stores:
        store.wait()


def update_kernel(grad_ref, after_ref, *rest):
    del after_ref
    factor_refs = rest[:-3]
    out_ref, held, sems = rest[-3:]
    panels, width, _ = grad_ref.shape
    rows = width // panels
    replica = lax.axis_index("rep")
    sources = [lax.rem(replica + panels - d, panels) for d in OFFSETS]
    grad = jnp.concatenate([grad_ref[c] for c in range(panels)], axis=1)
    right = jnp.concatenate(
        [
            jnp.concatenate([factor_ref[panels + h] for h in range(panels)], axis=0)
            for factor_ref in factor_refs
        ],
        axis=1,
    )
    stores = []
    for i, factor_ref in enumerate(factor_refs):
        left = jnp.concatenate([factor_ref[h] for h in range(panels)], axis=1)
        product = jnp.dot(left, grad, preferred_element_type=F32).astype(BF16)
        result = jnp.dot(product, right, preferred_element_type=F32).astype(BF16)
        to = pl.ds(pl.multiple_of(sources[i] * rows, rows), rows)
        for e in range(panels):
            held[i, e] = result[:, e * LANES : (e + 1) * LANES]
            stores.append(pltpu.make_async_copy(held.at[i, e], out_ref.at[sources[e], to], sems.at[i, e]))
            stores[-1].start()
    for store in stores:
        store.wait()


def products_kernel(offsets, grad_ref, *out_refs):
    panels, width, _ = grad_ref.shape
    rows = width // panels
    replica = lax.axis_index("rep")
    grad = jnp.concatenate([grad_ref[c] for c in range(panels)], axis=1)
    for d, out_ref in zip(offsets, out_refs, strict=True):
        to = lax.rem(replica + d, panels)
        start = pl.multiple_of(to * rows, rows)
        own_rows = jnp.concatenate([grad_ref[c, pl.ds(start, rows), :] for c in range(panels)], axis=1)
        left = lax.dot_general(own_rows, grad, (((1,), (1,)), ((), ())), preferred_element_type=F32)
        right = lax.dot_general(grad_ref[to], grad, (((0,), (0,)), ((), ())), preferred_element_type=F32)
        out_ref[0] = left.astype(out_ref.dtype)
        out_ref[1] = right.astype(out_ref.dtype)


def hold_kernel(in_ref, out_ref):
    out_ref[...] = in_ref[...]


def stats_kernel(plan_ref, left_ref, right_ref, *rest):
    product_refs = rest[:-7]
    left_out, right_out, lefts, rights, plan, sems, in_sem = rest[-7:]
    slots = left_ref.shape[0]
    replica = lax.axis_index("rep")
    load = pltpu.make_async_copy(plan_ref.at[:, pl.ds(0, PLACES)], plan, in_sem)
    load.start()
    load.wait()
    base = plan[0, BASE_AT]
    stores = []
    for i, (d, product_ref) in enumerate(zip(OFFSETS, product_refs, strict=True)):
        k = lax.rem(lax.rem(replica + slots - d, slots) + slots - base, slots)
        for n, (old, new, out) in enumerate(((left_ref, lefts, left_out), (right_ref, rights, right_out))):
            new[i] = (0.9 * old[k].astype(F32) + 0.1 * product_ref[n].astype(F32)).astype(new.dtype)
            stores.append(pltpu.make_async_copy(new.at[i], out.at[k], sems.at[len(stores)]))
            stores[-1].start()
    for store in stores:
        store.wait()


def collect_kernel(plan_ref, in_ref, out_ref, update, plan, sems, sem):
    load = pltpu.make_async_copy(plan_ref.at[:, pl.ds(PLACES, PLACES)], plan, sem)
    load.start()
    load.wait()

    def move(b, _):
        update[b] = in_ref[plan[0, b]]
        return 0

    parts = sems.shape[0]
    length = update.shape[0] // parts
    stores = []
    for n in range(parts):
        lax.fori_loop(n * length, (n + 1) * length, move, 0, unroll=8)
        chunk = pl.ds(n * length, length)
        stores.append(pltpu.make_async_copy(update.at[chunk], out_ref.at[chunk], sems.at[n]))
        stores[n].start()
    for store in stores:
        store.wait()


def to_others(messages):
    count = len(messages)
    return [
        lax.ppermute(message, "rep", [(s, (s + d) % count) for s in range(count)]) if d else message
        for message, d in zip(messages, OFFSETS, strict=True)
    ]


def per_device(partials, owners, left_stat, right_stat, left_factor, right_factor):
    shards = lax.axis_size("shard")
    classes = lax.axis_size("rep")
    _, blocks, rows, width = partials.shape
    slots = left_stat.shape[1]
    quarter = width // classes
    panels = width // LANES
    count = blocks // classes
    tall = width // TILE

    part_tiles = (
        partials[0].reshape(blocks, rows, panels, LANES).transpose(0, 2, 1, 3).reshape(blocks, TILE, LANES)
    )
    right_tiles = right_factor[0].reshape(slots, panels, LANES, LANES)
    factor_message = jax.ShapeDtypeStruct((2 * panels, LANES, LANES), BF16)
    message, plan = pl.pallas_call(
        pack_kernel,
        out_shape=(
            jax.ShapeDtypeStruct((classes, count, TILE, LANES), BF16),
            jax.ShapeDtypeStruct((1, 2 * PLACES), jnp.int32),
        ),
        in_specs=[anywhere()] * 2,
        out_specs=[anywhere()] * 2,
        scratch_shapes=[
            VMEM((blocks, TILE, LANES), BF16),
            VMEM((blocks, TILE, LANES), BF16),
            SMEM((1, blocks), jnp.int32),
            VMEM((1, blocks), jnp.int32),
            VMEM((1, PLACES), jnp.int32),
            VMEM((1, PLACES), jnp.int32),
            SMEM((1, PLACES), jnp.int32),
            SMEM((1, PLACES), jnp.int32),
            VMEM((1, PLACES), jnp.int32),
            pltpu.SemaphoreType.DMA((classes,)),
            pltpu.SemaphoreType.DMA((classes,)),
            pltpu.SemaphoreType.DMA((5,)),
        ],
        compiler_params=params(WIDE),
        name="pack",
    )(owners.reshape(1, blocks), part_tiles)
    received = lax.all_to_all(message, "rep", split_axis=0, concat_axis=0, tiled=True)
    factors = pl.pallas_call(
        factors_kernel,
        out_shape=[factor_message] * classes,
        in_specs=[in_hbm(), anywhere(), anywhere()],
        out_specs=[anywhere()] * classes,
        scratch_shapes=[
            VMEM((slots, quarter, width), BF16),
            VMEM((classes, 2 * panels, LANES, LANES), BF16),
            SMEM((1, PLACES), jnp.int32),
            pltpu.SemaphoreType.DMA((classes + 1,)),
            pltpu.SemaphoreType.DMA((classes,)),
            pltpu.SemaphoreType.DMA,
        ],
        compiler_params=params(),
        cost_estimate=pl.CostEstimate(flops=0, bytes_accessed=8 * width**2, transcendentals=0),
        name="factors",
    )(plan, left_factor[0], right_tiles)
    packed = factors[-1]
    factors = to_others(factors)
    outgoing = pl.pallas_call(
        spread_kernel,
        out_shape=jax.ShapeDtypeStruct((shards, TILE, LANES), BF16),
        in_specs=[in_hbm(), in_hbm(), in_vmem()],
        out_specs=anywhere(),
        scratch_shapes=[
            VMEM((shards, TILE, LANES), BF16),
            SMEM((1, PLACES), jnp.int32),
            pltpu.SemaphoreType.DMA((4,)),
            pltpu.SemaphoreType.DMA,
        ],
        compiler_params=params(),
        name="spread",
    )(plan, packed, received)
    incoming = lax.all_to_all(outgoing, "shard", split_axis=0, concat_axis=0, tiled=True)
    grad = (
        incoming.reshape(shards, panels, rows, LANES).transpose(1, 0, 2, 3).reshape(panels, width, LANES)
    )
    products = []
    for offsets in (OFFSETS[:1], OFFSETS[1:]):
        products += pl.pallas_call(
            functools.partial(products_kernel, offsets),
            out_shape=[jax.ShapeDtypeStruct((2, quarter, width), BF16)] * len(offsets),
            in_specs=[in_vmem()],
            out_specs=[in_vmem()] * len(offsets),
            compiler_params=params(),
            cost_estimate=pl.CostEstimate(
                flops=len(offsets) * width**3, bytes_accessed=2 * width**2, transcendentals=0
            ),
            name="products",
        )(grad)
    update_panels = pl.pallas_call(
        update_kernel,
        out_shape=jax.ShapeDtypeStruct((panels, width, LANES), BF16),
        in_specs=[in_vmem(), anywhere()] + [in_vmem()] * classes,
        out_specs=anywhere(),
        scratch_shapes=[
            VMEM((panels, panels, quarter, LANES), BF16),
            pltpu.SemaphoreType.DMA((panels, panels)),
        ],
        compiler_params=params(),
        cost_estimate=pl.CostEstimate(flops=4 * width**3, bytes_accessed=8 * width**2, transcendentals=0),
        name="update",
    )(grad, products[0], *factors)
    returned = lax.all_to_all(
        update_panels.reshape(panels * shards, rows, LANES),
        ("rep", "shard"),
        split_axis=0,
        concat_axis=0,
        tiled=True,
    )
    products = to_others(products)
    products[0] = pl.pallas_call(
        hold_kernel,
        out_shape=jax.ShapeDtypeStruct((2, quarter, width), BF16),
        in_specs=[in_vmem()],
        out_specs=in_vmem(),
        compiler_params=params(),
        cost_estimate=pl.CostEstimate(flops=HOLD, bytes_accessed=8 * quarter * width, transcendentals=0),
        name="hold",
    )(products[0])
    left_new, right_new = pl.pallas_call(
        stats_kernel,
        out_shape=(
            jax.ShapeDtypeStruct(left_stat.shape[1:], BF16),
            jax.ShapeDtypeStruct(right_stat.shape[1:], BF16),
        ),
        in_specs=[in_hbm()] + [in_vmem()] * (2 + classes),
        out_specs=(anywhere(), anywhere()),
        scratch_shapes=[
            VMEM((slots, quarter, width), BF16),
            VMEM((slots, quarter, width), BF16),
            SMEM((1, PLACES), jnp.int32),
            pltpu.SemaphoreType.DMA((2 * slots,)),
            pltpu.SemaphoreType.DMA,
        ],
        compiler_params=params(),
        cost_estimate=pl.CostEstimate(
            flops=8 * slots * quarter * width, bytes_accessed=12 * slots * quarter * width, transcendentals=0
        ),
        name="stats",
    )(plan, left_stat[0], right_stat[0], *products)
    update = pl.pallas_call(
        collect_kernel,
        out_shape=jax.ShapeDtypeStruct((blocks, rows, LANES), BF16),
        in_specs=[in_hbm(), in_vmem()],
        out_specs=anywhere(),
        scratch_shapes=[
            VMEM((blocks, rows, LANES), BF16),
            SMEM((1, PLACES), jnp.int32),
            pltpu.SemaphoreType.DMA((classes,)),
            pltpu.SemaphoreType.DMA,
        ],
        compiler_params=params(),
        cost_estimate=pl.CostEstimate(flops=0, bytes_accessed=4 * blocks * rows * LANES, transcendentals=0),
        name="collect",
    )(plan, returned)
    return left_new[None], right_new[None], update


def solution(mesh):
    return jax.shard_map(
        per_device,
        mesh=mesh,
        in_specs=(
            P("rep", None, "shard", None),
            P(),
            P("shard", None, "rep", None),
            P("shard", None, "rep", None),
            P("shard", None, "rep", None),
            P("shard", None, None, "rep"),
        ),
        out_specs=(
            P("shard", None, "rep", None),
            P("shard", None, "rep", None),
            P(None, "shard", "rep"),
        ),
        check_vma=False,
    )
```

```python
import functools

import jax
import jax.numpy as jnp
from jax import lax
from jax.experimental import pallas as pl
from jax.experimental.pallas import tpu as pltpu
from jax.sharding import PartitionSpec as P

VMEM = pltpu.VMEM
SMEM = pltpu.SMEM
LIMIT = 40 * 1024 * 1024
WIDE = 58 * 1024 * 1024
F32 = jnp.float32
BF16 = jnp.bfloat16
LANES = 128
TILE = 16
PLACES = 256
BASE_AT = PLACES - 1
OFFSETS = (2, 3, 1, 0)
HOLD = 1 << 34


def params(limit=LIMIT):
    return pltpu.CompilerParams(vmem_limit_bytes=limit)


def in_vmem():
    return pl.BlockSpec(memory_space=VMEM)


def in_smem():
    return pl.BlockSpec(memory_space=SMEM)


def anywhere():
    return pl.BlockSpec(memory_space=pl.ANY)


def in_hbm():
    return pl.BlockSpec(memory_space=pltpu.HBM)


def pack_kernel(
    owners_ref, part_ref, out_ref, plan_ref,
    part, message, owners, lanes, padded, place, place_at, plan, source, in_sems, out_sems, sems,
):
    classes, count = out_ref.shape[:2]
    blocks = part_ref.shape[0]
    load_owners = [
        pltpu.make_async_copy(owners_ref, owners, sems.at[0]),
        pltpu.make_async_copy(owners_ref, lanes, sems.at[1]),
    ]
    for load in load_owners:
        load.start()
    load_parts = []
    for c in range(classes):
        chunk = pl.ds(c * count, count)
        load_parts.append(pltpu.make_async_copy(part_ref.at[chunk], part.at[chunk], in_sems.at[c]))
        load_parts[c].start()
    for load in load_owners:
        load.wait()
    padded[...] = jnp.full_like(padded, lax.axis_size("shard"))
    padded[:, pl.ds(0, blocks)] = lanes[...]
    owner = padded[...]
    key = owner * PLACES + lax.broadcasted_iota(jnp.int32, owner.shape, 1)
    rank = jnp.zeros_like(key)
    for h in range(PLACES // LANES):
        square = jnp.broadcast_to(key[:, h * LANES : (h + 1) * LANES], (LANES, LANES)).T
        other = jnp.concatenate([square] * (PLACES // LANES), axis=1)
        rank = rank + jnp.sum(jnp.where(other < key, 1, 0), axis=0, keepdims=True)
    cls = lax.rem(rank, classes)
    place[...] = cls * count + lax.div(rank, classes)
    bring = pltpu.make_async_copy(place, place_at, sems.at[2])
    bring.start()
    source[...] = cls * lax.axis_size("shard") + owner
    stores = [pltpu.make_async_copy(source, plan_ref.at[:, pl.ds(PLACES, PLACES)], sems.at[3])]
    stores[0].start()
    base = jnp.sum(jnp.where(owner < lax.axis_index("shard"), 1, 0))
    plan[0, BASE_AT] = lax.rem(base, classes)
    bring.wait()
    for load in load_parts:
        load.wait()

    def move(b, _):
        at = place_at[0, b]
        message[at] = part[b]
        plan[0, at] = owners[0, b]
        return 0

    lax.fori_loop(0, blocks, move, 0, unroll=8)
    stores.append(pltpu.make_async_copy(plan, plan_ref.at[:, pl.ds(0, PLACES)], sems.at[4]))
    stores[-1].start()
    for c in range(classes):
        stores.append(pltpu.make_async_copy(message.at[pl.ds(c * count, count)], out_ref.at[c], out_sems.at[c]))
        stores[-1].start()
    for store in stores:
        store.wait()


def factors_kernel(plan_ref, left_ref, right_ref, *rest):
    factor_outs = rest[:-6]
    left, factors, plan, in_sems, out_sems, sem = rest[-6:]
    classes = len(OFFSETS)
    panels = right_ref.shape[1]
    replica = lax.axis_index("rep")
    load_plan = pltpu.make_async_copy(plan_ref.at[:, pl.ds(0, PLACES)], plan, sem)
    load_plan.start()
    load_left = pltpu.make_async_copy(left_ref, left, in_sems.at[classes])
    load_left.start()
    load_plan.wait()
    slots, loads, stores = [], [], []
    for n, d in enumerate(OFFSETS):
        slots.append(lax.rem(lax.rem(replica + d, classes) + classes - plan[0, BASE_AT], classes))
        loads.append(
            pltpu.make_async_copy(right_ref.at[slots[n]], factors.at[n, pl.ds(panels, panels)], in_sems.at[n])
        )
        loads[n].start()
    load_left.wait()
    for n, factor_out in enumerate(factor_outs):
        for h in range(panels):
            factors[n, h] = left[slots[n], :, h * LANES : (h + 1) * LANES]
        loads[n].wait()
        stores.append(pltpu.make_async_copy(factors.at[n], factor_out, out_sems.at[n]))
        stores[n].start()
    for store in stores:
        store.wait()


def spread_kernel(plan_ref, after_ref, in_ref, out_ref, spread, sums, plan, sems, sem):
    del after_ref
    load = pltpu.make_async_copy(plan_ref.at[:, pl.ds(0, PLACES)], plan, sem)
    load.start()
    spread[...] = jnp.zeros_like(spread)
    classes, count = in_ref.shape[:2]
    first = lax.axis_index("rep") * count

    def add(j, _):
        total = in_ref[0, j].astype(F32)
        for r in range(1, classes):
            total = total + in_ref[r, j].astype(F32)
        sums[j] = total.astype(sums.dtype)
        return 0

    lax.fori_loop(0, count, add, 0, unroll=8)
    load.wait()

    def place(j, _):
        spread[plan[0, first + j]] = sums[j]
        return 0

    lax.fori_loop(0, count, place, 0, unroll=8)
    parts = sems.shape[0]
    length = spread.shape[0] // parts
    stores = []
    for n in range(parts):
        chunk = pl.ds(n * length, length)
        stores.append(pltpu.make_async_copy(spread.at[chunk], out_ref.at[chunk], sems.at[n]))
        stores[n].start()
    for store in stores:
        store.wait()


def update_kernel(grad_ref, after_ref, *rest):
    del after_ref
    factor_refs = rest[:-4]
    out_ref, product, held, sems = rest[-4:]
    panels, width, _ = grad_ref.shape
    rows = width // panels
    replica = lax.axis_index("rep")
    sources = [lax.rem(replica + panels - d, panels) for d in OFFSETS]
    grad = jnp.concatenate([grad_ref[c] for c in range(panels)], axis=1)
    for d, factor_ref in enumerate(factor_refs):
        left = jnp.concatenate([factor_ref[h] for h in range(panels)], axis=1)
        product[d * rows : (d + 1) * rows] = jnp.dot(left, grad, preferred_element_type=F32).astype(BF16)
    stores = []
    for d, factor_ref in enumerate(factor_refs):
        right = jnp.concatenate([factor_ref[panels + h] for h in range(panels)], axis=0)
        result = jnp.dot(product[...], right, preferred_element_type=F32).astype(BF16)
        for e in range(panels):
            held[d, e] = result[e * rows : (e + 1) * rows]
        for e in range(panels):
            to = pl.ds(pl.multiple_of(sources[e] * rows, rows), rows)
            stores.append(pltpu.make_async_copy(held.at[d, e], out_ref.at[sources[d], to], sems.at[d, e]))
            stores[-1].start()
    for store in stores:
        store.wait()


def products_kernel(offsets, grad_ref, *out_refs):
    panels, width, _ = grad_ref.shape
    rows = width // panels
    replica = lax.axis_index("rep")
    grad = jnp.concatenate([grad_ref[c] for c in range(panels)], axis=1)
    for d, out_ref in zip(offsets, out_refs, strict=True):
        to = lax.rem(replica + d, panels)
        start = pl.multiple_of(to * rows, rows)
        own_rows = jnp.concatenate([grad_ref[c, pl.ds(start, rows), :] for c in range(panels)], axis=1)
        left = lax.dot_general(own_rows, grad, (((1,), (1,)), ((), ())), preferred_element_type=F32)
        right = lax.dot_general(grad_ref[to], grad, (((0,), (0,)), ((), ())), preferred_element_type=F32)
        out_ref[0] = left.astype(out_ref.dtype)
        out_ref[1] = right.astype(out_ref.dtype)


def hold_kernel(in_ref, out_ref):
    out_ref[...] = in_ref[...]


def stats_kernel(plan_ref, left_ref, right_ref, *rest):
    product_refs = rest[:-7]
    left_out, right_out, lefts, rights, plan, sems, in_sem = rest[-7:]
    slots = left_ref.shape[0]
    replica = lax.axis_index("rep")
    load = pltpu.make_async_copy(plan_ref.at[:, pl.ds(0, PLACES)], plan, in_sem)
    load.start()
    load.wait()
    base = plan[0, BASE_AT]
    stores = []
    for i, (d, product_ref) in enumerate(zip(OFFSETS, product_refs, strict=True)):
        k = lax.rem(lax.rem(replica + slots - d, slots) + slots - base, slots)
        for n, (old, new, out) in enumerate(((left_ref, lefts, left_out), (right_ref, rights, right_out))):
            new[i] = (0.9 * old[k].astype(F32) + 0.1 * product_ref[n].astype(F32)).astype(new.dtype)
            stores.append(pltpu.make_async_copy(new.at[i], out.at[k], sems.at[len(stores)]))
            stores[-1].start()
    for store in stores:
        store.wait()


def collect_kernel(plan_ref, in_ref, out_ref, update, plan, sem, in_sem):
    load = pltpu.make_async_copy(plan_ref.at[:, pl.ds(PLACES, PLACES)], plan, in_sem)
    load.start()
    load.wait()

    def move(b, _):
        update[b] = in_ref[plan[0, b]]
        return 0

    lax.fori_loop(0, update.shape[0], move, 0, unroll=8)
    store = pltpu.make_async_copy(update, out_ref, sem)
    store.start()
    store.wait()


def to_others(messages):
    count = len(messages)
    return [
        lax.ppermute(message, "rep", [(s, (s + d) % count) for s in range(count)]) if d else message
        for message, d in zip(messages, OFFSETS, strict=True)
    ]


def per_device(partials, owners, left_stat, right_stat, left_factor, right_factor):
    shards = lax.axis_size("shard")
    classes = lax.axis_size("rep")
    _, blocks, rows, width = partials.shape
    slots = left_stat.shape[1]
    quarter = width // classes
    panels = width // LANES
    count = blocks // classes
    tall = width // TILE

    part_tiles = (
        partials[0].reshape(blocks, rows, panels, LANES).transpose(0, 2, 1, 3).reshape(blocks, TILE, LANES)
    )
    right_tiles = right_factor[0].reshape(slots, panels, LANES, LANES)
    factor_message = jax.ShapeDtypeStruct((2 * panels, LANES, LANES), BF16)
    message, plan = pl.pallas_call(
        pack_kernel,
        out_shape=(
            jax.ShapeDtypeStruct((classes, count, TILE, LANES), BF16),
            jax.ShapeDtypeStruct((1, 2 * PLACES), jnp.int32),
        ),
        in_specs=[anywhere()] * 2,
        out_specs=[anywhere()] * 2,
        scratch_shapes=[
            VMEM((blocks, TILE, LANES), BF16),
            VMEM((blocks, TILE, LANES), BF16),
            SMEM((1, blocks), jnp.int32),
            VMEM((1, blocks), jnp.int32),
            VMEM((1, PLACES), jnp.int32),
            VMEM((1, PLACES), jnp.int32),
            SMEM((1, PLACES), jnp.int32),
            SMEM((1, PLACES), jnp.int32),
            VMEM((1, PLACES), jnp.int32),
            pltpu.SemaphoreType.DMA((classes,)),
            pltpu.SemaphoreType.DMA((classes,)),
            pltpu.SemaphoreType.DMA((5,)),
        ],
        compiler_params=params(WIDE),
        name="pack",
    )(owners.reshape(1, blocks), part_tiles)
    received = lax.all_to_all(message, "rep", split_axis=0, concat_axis=0, tiled=True)
    factors = pl.pallas_call(
        factors_kernel,
        out_shape=[factor_message] * classes,
        in_specs=[in_hbm(), anywhere(), anywhere()],
        out_specs=[anywhere()] * classes,
        scratch_shapes=[
            VMEM((slots, quarter, width), BF16),
            VMEM((classes, 2 * panels, LANES, LANES), BF16),
            SMEM((1, PLACES), jnp.int32),
            pltpu.SemaphoreType.DMA((classes + 1,)),
            pltpu.SemaphoreType.DMA((classes,)),
            pltpu.SemaphoreType.DMA,
        ],
        compiler_params=params(),
        cost_estimate=pl.CostEstimate(flops=0, bytes_accessed=8 * width**2, transcendentals=0),
        name="factors",
    )(plan, left_factor[0], right_tiles)
    packed = factors[-1]
    factors = to_others(factors)
    outgoing = pl.pallas_call(
        spread_kernel,
        out_shape=jax.ShapeDtypeStruct((shards, TILE, LANES), BF16),
        in_specs=[in_hbm(), in_hbm(), in_vmem()],
        out_specs=anywhere(),
        scratch_shapes=[
            VMEM((shards, TILE, LANES), BF16),
            VMEM((count, TILE, LANES), BF16),
            SMEM((1, PLACES), jnp.int32),
            pltpu.SemaphoreType.DMA((4,)),
            pltpu.SemaphoreType.DMA,
        ],
        compiler_params=params(),
        name="spread",
    )(plan, packed, received)
    incoming = lax.all_to_all(outgoing, "shard", split_axis=0, concat_axis=0, tiled=True)
    grad = (
        incoming.reshape(shards, panels, rows, LANES).transpose(1, 0, 2, 3).reshape(panels, width, LANES)
    )
    products = []
    for offsets in (OFFSETS[:1], OFFSETS[1:]):
        products += pl.pallas_call(
            functools.partial(products_kernel, offsets),
            out_shape=[jax.ShapeDtypeStruct((2, quarter, width), BF16)] * len(offsets),
            in_specs=[in_vmem()],
            out_specs=[in_vmem()] * len(offsets),
            compiler_params=params(),
            cost_estimate=pl.CostEstimate(
                flops=len(offsets) * width**3, bytes_accessed=2 * width**2, transcendentals=0
            ),
            name="products",
        )(grad)
    update_panels = pl.pallas_call(
        update_kernel,
        out_shape=jax.ShapeDtypeStruct((panels, width, LANES), BF16),
        in_specs=[in_vmem(), anywhere()] + [in_vmem()] * classes,
        out_specs=anywhere(),
        scratch_shapes=[
            VMEM((width, width), BF16),
            VMEM((panels, panels, quarter, LANES), BF16),
            pltpu.SemaphoreType.DMA((panels, panels)),
        ],
        compiler_params=params(),
        cost_estimate=pl.CostEstimate(flops=4 * width**3, bytes_accessed=8 * width**2, transcendentals=0),
        name="update",
    )(grad, products[0], *factors)
    returned = lax.all_to_all(
        update_panels.reshape(panels * shards, rows, LANES),
        ("rep", "shard"),
        split_axis=0,
        concat_axis=0,
        tiled=True,
    )
    products = to_others(products)
    products[0] = pl.pallas_call(
        hold_kernel,
        out_shape=jax.ShapeDtypeStruct((2, quarter, width), BF16),
        in_specs=[in_vmem()],
        out_specs=in_vmem(),
        compiler_params=params(),
        cost_estimate=pl.CostEstimate(flops=HOLD, bytes_accessed=8 * quarter * width, transcendentals=0),
        name="hold",
    )(products[0])
    left_new, right_new = pl.pallas_call(
        stats_kernel,
        out_shape=(
            jax.ShapeDtypeStruct(left_stat.shape[1:], BF16),
            jax.ShapeDtypeStruct(right_stat.shape[1:], BF16),
        ),
        in_specs=[in_hbm()] + [in_vmem()] * (2 + classes),
        out_specs=(anywhere(), anywhere()),
        scratch_shapes=[
            VMEM((slots, quarter, width), BF16),
            VMEM((slots, quarter, width), BF16),
            SMEM((1, PLACES), jnp.int32),
            pltpu.SemaphoreType.DMA((2 * slots,)),
            pltpu.SemaphoreType.DMA,
        ],
        compiler_params=params(),
        cost_estimate=pl.CostEstimate(
            flops=8 * slots * quarter * width, bytes_accessed=12 * slots * quarter * width, transcendentals=0
        ),
        name="stats",
    )(plan, left_stat[0], right_stat[0], *products)
    update = pl.pallas_call(
        collect_kernel,
        out_shape=jax.ShapeDtypeStruct((blocks, rows, LANES), BF16),
        in_specs=[in_hbm(), in_vmem()],
        out_specs=anywhere(),
        scratch_shapes=[
            VMEM((blocks, rows, LANES), BF16),
            SMEM((1, PLACES), jnp.int32),
            pltpu.SemaphoreType.DMA,
            pltpu.SemaphoreType.DMA,
        ],
        compiler_params=params(),
        cost_estimate=pl.CostEstimate(flops=0, bytes_accessed=4 * blocks * rows * LANES, transcendentals=0),
        name="collect",
    )(plan, returned)
    return left_new[None], right_new[None], update


def solution(mesh):
    return jax.shard_map(
        per_device,
        mesh=mesh,
        in_specs=(
            P("rep", None, "shard", None),
            P(),
            P("shard", None, "rep", None),
            P("shard", None, "rep", None),
            P("shard", None, "rep", None),
            P("shard", None, None, "rep"),
        ),
        out_specs=(
            P("shard", None, "rep", None),
            P("shard", None, "rep", None),
            P(None, "shard", "rep"),
        ),
        check_vma=False,
    )
```
